32 devices in a mesh: req: 2 (over y), row: 4 (over z), col: 4 (over x, core).
Axes of the slice: x: 2, y: 2, z: 4, core: 2. Of those that a mesh axis runs over, the one named last changes fastest.
Arguments:
- tokens: bfloat16 [4096, 1024], P(('req', 'row')), may hold values from -6 to 6
- norm_gain: float32 [1024], replicated, may hold values from 0.5 to 1.5
- w_attn: bfloat16 [5, 1024, 1024], P(None, 'row', 'col'), may hold values from -1 to 1
- persist_kv: bfloat16 [2, 16, 1024], P(None, None, 'col'), may hold values from -6 to 6
- kv_pool: bfloat16 [8, 8, 4, 256, 2, 1024], P(('req', 'row'), None, None, None, None, 'col'), may hold values from -6 to 6
- cache_len: int32 [8], replicated, may hold values from 0 to 8192, as said below
- mem_state: float32 [8, 8, 128, 128], P(('req', 'row'), 'col'), may hold values from -0.5 to 0.5
- decay: float32 [8, 8, 8], P(('req', 'row'), None, 'col'), may hold values from 0.6 to 1
- rate: float32 [8, 8, 8], P(('req', 'row'), None, 'col'), may hold values from 0.05 to 0.5
Outputs:
- mixed: bfloat16 [4096, 1024], P(('req', 'row'), 'col')
- new_state: float32 [8, 8, 128, 128], P(('req', 'row'), 'col')
The draws below stay inside these ranges and needn't reach their ends.
Inputs may be any that keep to these rules, and one draw needn't show every extreme that they name: `cache_len`: cached tokens before each block; some block has exactly 8192.
All inputs are finite; a program needn't handle non-finite values.
Results may differ from the reference program's by a relative error of at most 0.006.
Values may be sent and summed in bfloat16 or wider, within the bound.
No kernel may reach another device: no remote copies, remote signals or barrier semaphores. Data moves between devices by JAX's collectives and lax.ppermute only.
A program may use at most 192 MiB of HBM per device.

```python
import math
import jax
import jax.numpy as jnp
from jax import lax

D = 1024
H = 8
HD = 128
NP = 16
S = 512
SEG = 64
PAGE = 256
MAXP = 32
POOL = 8
SPANS = 8
MOST = 4
CACHE = 8192
NSEG = 8


def draw_cache_len(key, part):
    first_key, second_key = jax.random.split(key)
    lengths = jax.random.randint(first_key, (SPANS,), 0, CACHE + 1)
    chosen = jax.random.randint(second_key, (), 0, SPANS)
    return jnp.where(jnp.arange(SPANS) == chosen, CACHE, lengths).astype(jnp.int32)


def clipped_normal(key, shape):
    return jnp.clip(jax.random.normal(key, shape, dtype=jnp.float32), -6.0, 6.0)


def draw_tokens(key, part):
    rows_total = SPANS * S
    values = clipped_normal(jax.random.fold_in(key, 11), (rows_total, D))
    return values.astype(jnp.bfloat16)


def draw_w_attn(key, part):
    values = clipped_normal(jax.random.fold_in(key, 21), (5, D, D)) * D ** (-0.5)
    return values.astype(jnp.bfloat16)


def draw_persist_kv(key, part):
    values = clipped_normal(jax.random.fold_in(key, 31), (2, NP, D))
    return values.astype(jnp.bfloat16)


def draw_kv_pool(key, part):
    values = clipped_normal(jax.random.fold_in(key, 41), (POOL, SPANS, MOST, PAGE, 2, D))
    return values.astype(jnp.bfloat16)


def block_levels(rng, dims, cuts, smallest, high):
    loudness = 1.0
    for position, parts in cuts:
        draws = jax.random.uniform(jax.random.fold_in(jax.random.fold_in(rng, 6), position), (parts,), jnp.float32, smallest / len(cuts), high / len(cuts))
        loudness = loudness * jnp.repeat(jnp.exp(draws), dims[position] // parts).reshape((-1,) + (1,) * (len(dims) - 1 - position))
    return loudness


def bell_draw(own_key, shape, deviation, most, shards=(), held_as=jnp.bfloat16):
    drawn = deviation * jax.random.normal(own_key, shape, jnp.float32)
    if shards:
        drawn = drawn * block_levels(own_key, shape, shards, -0.22, 0.18)
    return jnp.clip(drawn, -most, most).astype(held_as)


def setup_inputs(seed: int = 0) -> dict:
    streams_of = jax.random.split(jax.random.key(seed), 10)
    return {
        "tokens": draw_tokens(jax.random.fold_in(streams_of[9], 71), 0),
        "norm_gain": jnp.clip(1.0 + 0.1 * jax.random.normal(streams_of[1], (D,), jnp.float32), 0.5, 1.5),
        "w_attn": draw_w_attn(jax.random.fold_in(streams_of[9], 71), 0),
        "persist_kv": draw_persist_kv(jax.random.fold_in(streams_of[9], 71), 0),
        "kv_pool": draw_kv_pool(jax.random.fold_in(streams_of[9], 71), 0),
        "cache_len": draw_cache_len(jax.random.fold_in(streams_of[9], 71), 0),
        "mem_state": bell_draw(streams_of[6], (SPANS, H, HD, HD), HD ** -0.5, 0.5, ((0, 8), (1, 4)), jnp.float32),
        "decay": jnp.clip(jnp.exp(math.log(1.0) - 0.5108256 * jax.random.uniform(streams_of[7], (SPANS, NSEG, H), jnp.float32) ** block_levels(streams_of[7], (SPANS, NSEG, H), ((0, 8), (2, 4)), -0.2, 0.2)), 0.6, 1.0),
        "rate": jnp.clip(jnp.exp(math.log(0.5) - 2.3025851 * jax.random.uniform(streams_of[8], (SPANS, NSEG, H), jnp.float32) ** block_levels(streams_of[8], (SPANS, NSEG, H), ((0, 8), (2, 4)), -0.2, 0.2)), 0.05, 0.5),
    }


negative_fill = -1e+30

def reference(tokens, norm_gain, w_attn, persist_kv, kv_pool, cache_len, mem_state, decay, rate):
    xfloat = tokens.astype(jnp.float32)
    normed = (xfloat * lax.rsqrt(lax.optimization_barrier(jnp.mean(xfloat * xfloat, axis=-1, keepdims=True)) + 1e-05) * norm_gain).astype(jnp.bfloat16)
    queries = jnp.dot(normed, w_attn[0], preferred_element_type=jnp.float32).astype(jnp.bfloat16)
    keys_new = jnp.dot(normed, w_attn[1], preferred_element_type=jnp.float32).astype(jnp.bfloat16)
    values_new = jnp.dot(normed, w_attn[2], preferred_element_type=jnp.float32).astype(jnp.bfloat16)
    gate_open = jax.nn.sigmoid(jnp.dot(normed, w_attn[3], preferred_element_type=jnp.float32))
    query_all = queries.reshape(SPANS, S, H, HD)
    keys_all = keys_new.reshape(SPANS, S, H, HD)
    values_all = values_new.reshape(SPANS, S, H, HD)
    persist_keys = persist_kv[0].reshape(NP, H, HD).astype(jnp.float32)
    persist_vals = persist_kv[1].reshape(NP, H, HD).astype(jnp.float32)
    scale_qk = HD ** (-0.5)
    causal = jnp.arange(S, dtype=jnp.int32)[:, None] >= jnp.arange(S, dtype=jnp.int32)[None, :]

    def one_span(span_index):
        device_ids = (span_index + jnp.arange(MAXP, dtype=jnp.int32)) % POOL
        slot_index = jnp.arange(MAXP, dtype=jnp.int32) // POOL
        page_data = kv_pool[device_ids, span_index, slot_index].reshape(CACHE, 2, H, HD).astype(jnp.float32)
        span_query = query_all[span_index].astype(jnp.float32)
        span_keys = keys_all[span_index].astype(jnp.float32)
        span_values = values_all[span_index].astype(jnp.float32)
        keys_cat = jnp.concatenate([persist_keys, page_data[:, 0], span_keys], axis=0)
        vals_cat = jnp.concatenate([persist_vals, page_data[:, 1], span_values], axis=0)
        cache_ok = jnp.arange(CACHE, dtype=jnp.int32) < cache_len[span_index]
        allowed = jnp.concatenate([jnp.ones((S, NP), dtype=bool), jnp.broadcast_to(cache_ok[None, :], (S, CACHE)), causal], axis=1)
        scores = jnp.einsum('shd,khd->hsk', span_query, keys_cat) * scale_qk
        scores = jnp.where(allowed[None], scores, negative_fill)
        maxima = lax.optimization_barrier(jnp.max(scores, axis=-1, keepdims=True))
        probabilities = jnp.where(allowed[None], jnp.exp(scores - maxima), 0.0)
        totals = lax.optimization_barrier(jnp.sum(probabilities, axis=-1))
        rounded = lax.optimization_barrier(probabilities.astype(jnp.bfloat16)).astype(jnp.float32)
        attended = jnp.einsum('hsk,khd->shd', rounded, vals_cat) / jnp.transpose(totals)[:, :, None]
        query_unit = span_query * lax.rsqrt(lax.optimization_barrier(jnp.sum(span_query * span_query, axis=-1, keepdims=True)) + 1e-06)
        key_unit = span_keys * lax.rsqrt(lax.optimization_barrier(jnp.sum(span_keys * span_keys, axis=-1, keepdims=True)) + 1e-06)
        memory = mem_state[span_index]
        span_decay = decay[span_index]
        span_rate = rate[span_index]
        outputs = []
        for segment in range(NSEG):
            lower = segment * SEG
            seg_query = query_unit[lower:lower + SEG]
            seg_keys = key_unit[lower:lower + SEG]
            seg_values = span_values[lower:lower + SEG]
            outputs.append(jnp.einsum('shd,hde->she', seg_query, memory, precision=lax.Precision.HIGHEST))
            errors = jnp.einsum('shd,hde->she', seg_keys, memory, precision=lax.Precision.HIGHEST) - seg_values
            update = jnp.einsum('shd,she->hde', seg_keys, errors, precision=lax.Precision.HIGHEST)
            memory = span_decay[segment][:, None, None] * memory - span_rate[segment][:, None, None] * update
        recalled = jnp.concatenate(outputs, axis=0)
        return (attended, recalled, memory)
    attended, recalled, new_state = lax.map(one_span, jnp.arange(SPANS, dtype=jnp.int32))
    combined = (attended.reshape(SPANS * S, D) + gate_open * recalled.reshape(SPANS * S, D)).astype(jnp.bfloat16)
    mixed = (xfloat + jnp.dot(combined, w_attn[4].T, preferred_element_type=jnp.float32)).astype(jnp.bfloat16)
    return (mixed, new_state)
```

```python
import functools

import jax
import jax.numpy as jnp
from jax import lax
from jax.experimental import pallas as pl
from jax.experimental.pallas import tpu as pltpu
from jax.sharding import PartitionSpec as P

HD = 128
NP = 16
SEG = 64
LOG2E = 1.4426950408889634
SCALE = HD ** (-0.5) * LOG2E
EMPTY = -1e30
STAT = 16
F32 = jnp.float32
BF16 = jnp.bfloat16
VMEM_LIMIT = 48 * 1024 * 1024


def nt(a, b):
    return lax.dot_general(a, b, (((1,), (1,)), ((), ())), preferred_element_type=F32)


def nn(a, b):
    return lax.dot_general(a, b, (((1,), (0,)), ((), ())), preferred_element_type=F32)


def split3(x):
    high = x.astype(BF16).astype(F32)
    rest = x - high
    middle = rest.astype(BF16).astype(F32)
    return high, middle, (rest - middle).astype(BF16).astype(F32)


def write_stats(out_ref, length, width, lse):
    lanes = lax.broadcasted_iota(jnp.int32, (length, 128), 1)
    table = jnp.zeros((length, 128), F32)
    place = 0
    for column in lse:
        for piece in split3(column):
            table = jnp.where(lanes == place, piece, table)
            place += 1
    rows = jnp.transpose(table)[:8]
    parts = length // width
    packed = jnp.concatenate(
        [rows[:, part * width : (part + 1) * width] for part in range(parts)], axis=0
    )
    out_ref[length : length + 8 * parts, :] = packed.astype(BF16)


def read_stats(ref, length, width, heads):
    parts = length // width
    packed = ref[length : length + 8 * parts, :].astype(F32)
    rows = jnp.concatenate([packed[8 * part : 8 * part + 8] for part in range(parts)], axis=1)
    rows = jnp.concatenate([rows, jnp.zeros((120, length), F32)], axis=0)
    table = jnp.transpose(rows)
    return [
        table[:, 3 * head : 3 * head + 1]
        + table[:, 3 * head + 1 : 3 * head + 2]
        + table[:, 3 * head + 2 : 3 * head + 3]
        for head in range(heads)
    ]


def project_kernel(place, normed, *refs):
    shards, out = refs[:-1], refs[-1]
    depth = shards[0].shape[0]
    count = len(shards)
    total = None
    for step in range(count):
        owner = lax.rem(place[0] - step + count, count)
        part = normed[:, pl.ds(pl.multiple_of(owner * depth, depth), depth)]
        term = nn(part, shards[step][...])
        total = term if total is None else total + term
    out[...] = total.astype(BF16)


def smem():
    return pl.BlockSpec(memory_space=pltpu.SMEM)


def vmem():
    return pl.BlockSpec(memory_space=pltpu.VMEM)


def params():
    return pltpu.CompilerParams(vmem_limit_bytes=VMEM_LIMIT)


def cost(flops, nbytes):
    return pl.CostEstimate(flops=flops, bytes_accessed=nbytes, transcendentals=0)


def project(place, normed, shards):
    length, width = normed.shape[0], shards[0].shape[1]
    return pl.pallas_call(
        project_kernel,
        out_shape=jax.ShapeDtypeStruct((length, width), BF16),
        in_specs=[smem()] + [vmem()] * (1 + len(shards)),
        out_specs=vmem(),
        compiler_params=params(),
        cost_estimate=cost(2 * length * normed.shape[1] * width, 2 * normed.size),
        name="project_queries",
    )(place, normed, *shards)


def pool_kernel(info, query, keys, values, out, *, slots, page, heads, length, width):
    used, remain = info[1], info[2]
    rows = 256
    half = length // rows

    @pl.when(used == 0)
    def _():
        out[:length, :] = jnp.zeros((length, width), BF16)
        write_stats(out, length, width, [jnp.full((length, 1), EMPTY, F32)] * heads)

    for count in range(1, slots + 1):

        @pl.when(used == count)
        def _(count=count):
            span = count * page
            columns = lax.broadcasted_iota(jnp.int32, (rows, page), 1)
            lse = []
            for head in range(heads):
                lanes = slice(head * HD, (head + 1) * HD)
                pieces = []
                for part in range(half):
                    rs = slice(part * rows, (part + 1) * rows)
                    scores = nt(query[rs, lanes], keys[0, :span, lanes])
                    last = jnp.where(columns < remain, scores[:, span - page :], EMPTY)
                    if count > 1:
                        scores = jnp.concatenate([scores[:, : span - page], last], axis=1)
                    else:
                        scores = last
                    top = jnp.max(scores, axis=1, keepdims=True)
                    probs = jnp.exp2((scores - top) * SCALE)
                    total = jnp.sum(probs, axis=1, keepdims=True)
                    mixed = nn(probs.astype(BF16), values[0, :span, lanes])
                    out[rs, lanes] = (mixed / total).astype(BF16)
                    pieces.append(top * SCALE + jnp.log2(total))
                lse.append(jnp.concatenate(pieces, axis=0))
            write_stats(out, length, width, lse)


def pool_attend(info, query, keys, values, slots, page):
    length, width = query.shape
    heads = width // HD
    span = slots * page
    kernel = functools.partial(
        pool_kernel, slots=slots, page=page, heads=heads, length=length, width=width
    )
    return pl.pallas_call(
        kernel,
        out_shape=jax.ShapeDtypeStruct((length + STAT, width), BF16),
        grid_spec=pltpu.PrefetchScalarGridSpec(
            num_scalar_prefetch=1,
            grid=(1,),
            in_specs=[
                pl.BlockSpec((length, width), lambda i, info: (0, 0)),
                pl.BlockSpec((1, span, width), lambda i, info: (info[0], 0, 0)),
                pl.BlockSpec((1, span, width), lambda i, info: (info[0], 0, 0)),
            ],
            out_specs=pl.BlockSpec((length + STAT, width), lambda i, info: (0, 0)),
        ),
        compiler_params=params(),
        cost_estimate=cost(4 * length * span * width, 4 * span * width),
        name="pool_attention",
    )(info, query, keys, values)


def merge(parts, lse):
    top = functools.reduce(jnp.maximum, lse)
    weights = [jnp.exp2(one - top) for one in lse]
    total = functools.reduce(jnp.add, weights)
    mixed = functools.reduce(jnp.add, [w * p for w, p in zip(weights, parts)])
    return mixed / total, top + jnp.log2(total)


def merge_kernel(*refs, length, width, heads):
    ins, out = refs[:-1], refs[-1]
    stats = [read_stats(ref, length, width, heads) for ref in ins]
    merged = []
    for head in range(heads):
        lanes = slice(head * HD, (head + 1) * HD)
        mixed, lse = merge(
            [ref[:length, lanes].astype(F32) for ref in ins], [s[head] for s in stats]
        )
        out[:length, lanes] = mixed.astype(BF16)
        merged.append(lse)
    write_stats(out, length, width, merged)


def merge_parts(parts, length, width):
    kernel = functools.partial(merge_kernel, length=length, width=width, heads=width // HD)
    return pl.pallas_call(
        kernel,
        out_shape=jax.ShapeDtypeStruct((length + STAT, width), BF16),
        in_specs=[vmem()] * len(parts),
        out_specs=vmem(),
        compiler_params=params(),
        cost_estimate=cost(length * width * 4, 2 * length * width * (len(parts) + 1)),
        name="merge_partials",
    )(*parts)


def hp(a, b, dims):
    return lax.dot_general(
        a, b, (dims, ((), ())), precision=lax.Precision.HIGHEST, preferred_element_type=F32
    )


def local_kernel(
    place, decay, rate, normed, query, persist, memory_in, *refs, count, length, width, heads
):
    shards = refs[:count]
    attended, lse_out, gated, memory_out, keys, values, gates, memory = refs[count:]
    depth = shards[0].shape[1]
    owners = [lax.rem(place[0] - step + count, count) for step in range(count)]
    parts = [normed[:, pl.ds(pl.multiple_of(o * depth, depth), depth)] for o in owners]

    def projected(which):
        return functools.reduce(
            jnp.add, [nn(parts[step], shards[step][which]) for step in range(count)]
        )

    keys[...] = projected(0).astype(BF16)
    values[...] = projected(1).astype(BF16)
    gates[...] = jax.nn.sigmoid(projected(2))
    rows = 256
    columns_lse = []
    for head in range(heads):
        lanes = slice(head * HD, (head + 1) * HD)
        pieces = []
        for part in range(length // rows):
            rs = slice(part * rows, (part + 1) * rows)
            span = (part + 1) * rows
            scores = nt(query[rs, lanes], keys[:span, lanes])
            own = part * rows + lax.broadcasted_iota(jnp.int32, (rows, span), 0)
            theirs = lax.broadcasted_iota(jnp.int32, (rows, span), 1)
            scores = jnp.where(own >= theirs, scores, EMPTY)
            fixed = nt(query[rs, lanes], persist[0, :, lanes])
            top = jnp.maximum(
                jnp.max(scores, axis=1, keepdims=True), jnp.max(fixed, axis=1, keepdims=True)
            )
            probs = jnp.exp2((scores - top) * SCALE)
            fixed_probs = jnp.exp2((fixed - top) * SCALE)
            total = jnp.sum(probs, axis=1, keepdims=True) + jnp.sum(
                fixed_probs, axis=1, keepdims=True
            )
            mixed = nn(probs.astype(BF16), values[:span, lanes]) + nn(
                fixed_probs.astype(BF16), persist[1, :, lanes]
            )
            attended[rs, lanes] = mixed / total
            pieces.append(top * SCALE + jnp.log2(total))
        columns_lse.append(jnp.concatenate(pieces, axis=0))
    lanes_at = lax.broadcasted_iota(jnp.int32, (length, 128), 1)
    table = jnp.zeros((length, 128), F32)
    for head in range(heads):
        table = jnp.where(lanes_at == head, columns_lse[head], table)
    lse_out[...] = table

    memory[...] = memory_in[0]

    def update(segment, carry):
        rs = pl.ds(pl.multiple_of(segment * SEG, SEG), SEG)
        for head in range(heads):
            lanes = slice(head * HD, (head + 1) * HD)
            seg_query = query[rs, lanes].astype(F32)
            seg_keys = keys[rs, lanes].astype(F32)
            seg_query = seg_query * lax.rsqrt(
                jnp.sum(seg_query * seg_query, axis=1, keepdims=True) + 1e-06
            )
            seg_keys = seg_keys * lax.rsqrt(
                jnp.sum(seg_keys * seg_keys, axis=1, keepdims=True) + 1e-06
            )
            state = memory[head]
            both = hp(jnp.concatenate([seg_query, seg_keys], axis=0), state, ((1,), (0,)))
            gated[rs, lanes] = gates[rs, lanes] * both[:SEG]
            errors = both[SEG:] - values[rs, lanes].astype(F32)
            change = hp(seg_keys, errors, ((0,), (0,)))
            memory[head] = decay[segment, head] * state - rate[segment, head] * change
        return carry

    lax.fori_loop(0, length // SEG, update, 0)
    memory_out[0] = memory[...]


def local_part(place, decay, rate, normed, query, persist, memory, shards):
    length, width = query.shape
    heads = width // HD
    count = len(shards)
    kernel = functools.partial(
        local_kernel, count=count, length=length, width=width, heads=heads
    )
    return pl.pallas_call(
        kernel,
        out_shape=(
            jax.ShapeDtypeStruct((length, width), F32),
            jax.ShapeDtypeStruct((length, 128), F32),
            jax.ShapeDtypeStruct((length, width), F32),
            jax.ShapeDtypeStruct(memory.shape, F32),
        ),
        in_specs=[smem()] * 3 + [vmem()] * (4 + count),
        out_specs=(vmem(),) * 4,
        scratch_shapes=[
            pltpu.VMEM((length, width), BF16),
            pltpu.VMEM((length, width), BF16),
            pltpu.VMEM((length, width), F32),
            pltpu.VMEM((heads, HD, HD), F32),
        ],
        compiler_params=params(),
        cost_estimate=cost(20 * length * normed.shape[1] * width, 8 * normed.size),
        name="local_part",
    )(place, decay, rate, normed, query, persist, memory, *shards)


def final_kernel(place, attended, lse_in, gated, *refs, count, parts, length, width, heads):
    ins = refs[:parts]
    shards = refs[parts : parts + count]
    send, keep, combined = refs[parts + count :]
    stats = [read_stats(ref, length, width, heads) for ref in ins]
    for head in range(heads):
        lanes = slice(head * HD, (head + 1) * HD)
        mixed, _ = merge(
            [attended[:, lanes]] + [ref[:length, lanes].astype(F32) for ref in ins],
            [lse_in[:, head : head + 1]] + [s[head] for s in stats],
        )
        combined[:, lanes] = (mixed + gated[:, lanes]).astype(BF16)
    for step in range(count):
        owner = lax.rem(place[0] - step + count, count)
        term = nt(combined[...], shards[step][...]).astype(BF16)
        other = lax.rem(owner + place[1], 2)
        spot = lax.div(owner, 2)

        @pl.when(other == 1)
        def _():
            send[spot] = term

        @pl.when(other == 0)
        def _():
            keep[spot] = term


def final_part(place, attended, lse, gated, parts, shards):
    length, width = attended.shape
    heads = width // HD
    count = len(shards)
    kernel = functools.partial(
        final_kernel,
        count=count,
        parts=len(parts),
        length=length,
        width=width,
        heads=heads,
    )
    half = jax.ShapeDtypeStruct((count // 2, length, shards[0].shape[0]), BF16)
    return pl.pallas_call(
        kernel,
        out_shape=(half, half),
        in_specs=[smem()] + [vmem()] * (3 + len(parts) + count),
        out_specs=(vmem(), vmem()),
        scratch_shapes=[pltpu.VMEM((length, width), BF16)],
        compiler_params=params(),
        cost_estimate=cost(2 * length * width * 1024, 12 * length * width),
        name="final_part",
    )(place, attended, lse, gated, *parts, *shards)


def shards(tokens, norm_gain, w_attn, persist_kv, kv_pool, cache_len, mem_state, decay, rate):
    req, row, col = lax.axis_size("req"), lax.axis_size("row"), lax.axis_size("col")
    pool_size = req * row
    my_req, my_row, my_col = lax.axis_index("req"), lax.axis_index("row"), lax.axis_index("col")
    my_index = my_req * row + my_row
    length = tokens.shape[0]
    width = w_attn.shape[2]

    def shift(x, axis, by):
        size = lax.axis_size(axis)
        return lax.ppermute(x, axis, [(i, (i + by) % size) for i in range(size)])

    w_query = w_attn[0]
    query_shards = [w_query] + [shift(w_query, "row", s) for s in range(1, row)]

    xfloat = tokens.astype(F32)
    normed = (
        xfloat * lax.rsqrt(jnp.mean(xfloat * xfloat, axis=-1, keepdims=True) + 1e-05) * norm_gain
    ).astype(BF16)
    slots, page = kv_pool.shape[2], kv_pool.shape[3]
    pages = kv_pool[0].reshape(pool_size, slots * page, 2, width)
    cache_keys, cache_vals = pages[:, :, 0], pages[:, :, 1]

    place = jnp.stack([my_row, my_col]).astype(jnp.int32)
    queries = project(place, normed, query_shards)

    def block_info(block):
        offset = (my_index - block) % pool_size
        limit = cache_len[block]
        page_count = (limit + page - 1) // page
        used = jnp.clip((page_count - offset + pool_size - 1) // pool_size, 0, slots)
        last = (used - 1) * pool_size + offset
        return jnp.stack([block, used, limit - last * page]).astype(jnp.int32)

    partials = {}
    by_row = [queries] + [shift(queries, "row", s) for s in range(1, row)]
    w_rest, queries_used = lax.optimization_barrier((w_attn[1:4], queries))
    w_out, _ = lax.optimization_barrier((w_attn[4], queries))
    rest_shards = [w_rest] + [shift(w_rest, "row", s) for s in range(1, row)]
    out_shards = [w_out] + [shift(w_out, "row", s) for s in range(1, row)]
    order = [0] + [s for s in (1, row - 1) if 0 < s < row]
    order = list(dict.fromkeys(order + list(range(row))))
    for s in order:
        for t in reversed(range(req)):
            here = by_row[s] if t == 0 else shift(by_row[s], "req", t)
            block = ((my_req - t) % req) * row + (my_row - s) % row
            partials[s, t] = pool_attend(
                block_info(block), here, cache_keys, cache_vals, slots, page
            )
    local_out, local_lse, gated, new_state = local_part(
        place,
        decay[0],
        rate[0],
        normed,
        queries,
        persist_kv,
        mem_state,
        rest_shards,
    )
    final = []
    for s in order:
        back = [partials[s, 0]] + [shift(partials[s, t], "req", -t) for t in range(1, req)]
        if s == 0:
            final += back
        else:
            final.append(shift(merge_parts(back, length, width), "row", -s))
    send, keep = final_part(place, local_out, local_lse, gated, final, out_shards)
    got = lax.ppermute(send, "col", [(i, i ^ 1) for i in range(col)])
    summed = keep.astype(F32) + got.astype(F32)
    spot = my_col // 2
    own = lax.dynamic_index_in_dim(summed, spot, 0, keepdims=False)
    mine = lax.dynamic_slice_in_dim(xfloat, my_col * own.shape[1], own.shape[1], 1) + own
    for step in range(1, col // 2):
        away = lax.dynamic_index_in_dim(summed, spot ^ step, 0, keepdims=False).astype(BF16)
        mine = mine + lax.ppermute(away, "col", [(i, i ^ (2 * step)) for i in range(col)]).astype(
            F32
        )
    return (mine.astype(BF16), new_state)


def solution(mesh):
    return jax.shard_map(
        shards,
        mesh=mesh,
        in_specs=(
            P(("req", "row"), None),
            P(),
            P(None, "row", "col"),
            P(None, None, "col"),
            P(("req", "row"), None, None, None, None, "col"),
            P(),
            P(("req", "row"), "col", None, None),
            P(("req", "row"), None, "col"),
            P(("req", "row"), None, "col"),
        ),
        out_specs=(P(("req", "row"), "col"), P(("req", "row"), "col", None, None)),
        check_vma=False,
    )
```

```python
import functools

import jax
import jax.numpy as jnp
from jax import lax
from jax.experimental import pallas as pl
from jax.experimental.pallas import tpu as pltpu
from jax.sharding import PartitionSpec as P

HD = 128
NP = 16
SEG = 64
LOG2E = 1.4426950408889634
SCALE = HD ** (-0.5) * LOG2E
EMPTY = -1e30
STAT = 16
F32 = jnp.float32
BF16 = jnp.bfloat16
VMEM_LIMIT = 16 * 1024 * 1024


def nt(a, b):
    return lax.dot_general(a, b, (((1,), (1,)), ((), ())), preferred_element_type=F32)


def nn(a, b):
    return lax.dot_general(a, b, (((1,), (0,)), ((), ())), preferred_element_type=F32)


def split3(x):
    high = x.astype(BF16).astype(F32)
    rest = x - high
    middle = rest.astype(BF16).astype(F32)
    return high, middle, (rest - middle).astype(BF16).astype(F32)


def write_stats(out_ref, length, width, lse):
    lanes = lax.broadcasted_iota(jnp.int32, (length, 128), 1)
    table = jnp.zeros((length, 128), F32)
    place = 0
    for column in lse:
        for piece in split3(column):
            table = jnp.where(lanes == place, piece, table)
            place += 1
    rows = jnp.transpose(table)[:8]
    parts = length // width
    packed = jnp.concatenate(
        [rows[:, part * width : (part + 1) * width] for part in range(parts)], axis=0
    )
    out_ref[length : length + 8 * parts, :] = packed.astype(BF16)


def read_stats(ref, length, width, heads):
    parts = length // width
    packed = ref[length : length + 8 * parts, :].astype(F32)
    rows = jnp.concatenate([packed[8 * part : 8 * part + 8] for part in range(parts)], axis=1)
    rows = jnp.concatenate([rows, jnp.zeros((120, length), F32)], axis=0)
    table = jnp.transpose(rows)
    return [
        table[:, 3 * head : 3 * head + 1]
        + table[:, 3 * head + 1 : 3 * head + 2]
        + table[:, 3 * head + 2 : 3 * head + 3]
        for head in range(heads)
    ]


def project_kernel(place, normed, *refs):
    shards, out = refs[:-1], refs[-1]
    depth = shards[0].shape[0]
    count = len(shards)
    total = None
    for step in range(count):
        owner = lax.rem(place[0] - step + count, count)
        part = normed[:, pl.ds(pl.multiple_of(owner * depth, depth), depth)]
        term = nn(part, shards[step][...])
        total = term if total is None else total + term
    out[...] = total.astype(BF16)


def smem():
    return pl.BlockSpec(memory_space=pltpu.SMEM)


def vmem():
    return pl.BlockSpec(memory_space=pltpu.VMEM)


def params():
    return pltpu.CompilerParams(vmem_limit_bytes=VMEM_LIMIT)


def cost():
    return pl.CostEstimate(flops=1, bytes_accessed=1, transcendentals=0)


def project(place, normed, shards):
    length, width = normed.shape[0], shards[0].shape[1]
    return pl.pallas_call(
        project_kernel,
        out_shape=jax.ShapeDtypeStruct((length, width), BF16),
        in_specs=[smem()] + [vmem()] * (1 + len(shards)),
        out_specs=vmem(),
        compiler_params=params(),
        cost_estimate=cost(),
        name="project_queries",
    )(place, normed, *shards)


def page_kernel(pages, out, buffers, sems):
    blocks = out.shape[0]

    def fetch(i):
        return pltpu.make_async_copy(pages.at[i], buffers.at[i % 3], sems.at[i % 3])

    for i in range(min(2, blocks)):
        fetch(i).start()
    for i in range(blocks):
        if i + 2 < blocks:
            fetch(i + 2).start()
        fetch(i).wait()
        out[i] = buffers[i % 3].reshape(out.shape[1:])


def lay_out_pages(pages):
    blocks, span, _, width = pages.shape
    return pl.pallas_call(
        page_kernel,
        out_shape=jax.ShapeDtypeStruct((blocks, span, 2 * width), BF16),
        in_specs=[pl.BlockSpec(memory_space=pltpu.HBM)],
        out_specs=vmem(),
        scratch_shapes=[
            pltpu.VMEM((3, span, 2, width), BF16),
            pltpu.SemaphoreType.DMA((3,)),
        ],
        compiler_params=params(),
        cost_estimate=cost(),
        name="lay_out_pages",
    )(pages)


def pool_kernel(info, query, cache, out, *, which, slots, page, heads, length, width):
    block, used, remain = info[which, 0], info[which, 1], info[which, 2]

    @pl.when(used == 0)
    def _():
        out[:length, :] = jnp.zeros((length, width), BF16)
        write_stats(out, length, width, [jnp.full((length, 1), EMPTY, F32)] * heads)

    for count in range(1, slots + 1):

        @pl.when(used == count)
        def _(count=count):
            span = count * page
            columns = lax.broadcasted_iota(jnp.int32, (length, page), 1)
            lse = []
            for head in range(heads):
                lanes = slice(head * HD, (head + 1) * HD)
                after = slice(width + head * HD, width + (head + 1) * HD)
                scores = nt(query[:, lanes], cache[block, :span, lanes])
                last = jnp.where(columns < remain, scores[:, span - page :], EMPTY)
                if count > 1:
                    scores = jnp.concatenate([scores[:, : span - page], last], axis=1)
                else:
                    scores = last
                top = jnp.max(scores, axis=1, keepdims=True)
                probs = jnp.exp2((scores - top) * SCALE)
                total = jnp.sum(probs, axis=1, keepdims=True)
                mixed = nn(probs.astype(BF16), cache[block, :span, after])
                out[:length, lanes] = (mixed / total).astype(BF16)
                lse.append(top * SCALE + jnp.log2(total))
            write_stats(out, length, width, lse)


def pool_attend(which, info, query, cache, slots, page):
    length, width = query.shape
    kernel = functools.partial(
        pool_kernel,
        which=which,
        slots=slots,
        page=page,
        heads=width // HD,
        length=length,
        width=width,
    )
    return pl.pallas_call(
        kernel,
        out_shape=jax.ShapeDtypeStruct((length + STAT, width), BF16),
        in_specs=[smem(), vmem(), vmem()],
        out_specs=vmem(),
        compiler_params=params(),
        cost_estimate=cost(),
        name="pool_attention",
    )(info, query, cache)


def merge(parts, lse):
    top = functools.reduce(jnp.maximum, lse)
    weights = [jnp.exp2(one - top) for one in lse]
    total = functools.reduce(jnp.add, weights)
    mixed = functools.reduce(jnp.add, [w * p for w, p in zip(weights, parts)])
    return mixed / total, top + jnp.log2(total)


def merge_kernel(*refs, length, width, heads):
    ins, out = refs[:-1], refs[-1]
    stats = [read_stats(ref, length, width, heads) for ref in ins]
    merged = []
    for head in range(heads):
        lanes = slice(head * HD, (head + 1) * HD)
        mixed, lse = merge(
            [ref[:length, lanes].astype(F32) for ref in ins], [s[head] for s in stats]
        )
        out[:length, lanes] = mixed.astype(BF16)
        merged.append(lse)
    write_stats(out, length, width, merged)


def merge_parts(parts, length, width):
    kernel = functools.partial(merge_kernel, length=length, width=width, heads=width // HD)
    return pl.pallas_call(
        kernel,
        out_shape=jax.ShapeDtypeStruct((length + STAT, width), BF16),
        in_specs=[vmem()] * len(parts),
        out_specs=vmem(),
        compiler_params=params(),
        cost_estimate=cost(),
        name="merge_partials",
    )(*parts)


def hp(a, b, dims):
    def halves(x):
        high = x.astype(BF16)
        return high, (x - high.astype(F32)).astype(BF16)

    def dot(x, y):
        return lax.dot_general(x, y, (dims, ((), ())), preferred_element_type=F32)

    a_high, a_low = halves(a)
    b_high, b_low = halves(b)
    return dot(a_high, b_high) + (dot(a_high, b_low) + dot(a_low, b_high))


def feature_parts(place, normed, count, depth):
    owners = [lax.rem(place[0] - step + count, count) for step in range(count)]
    return [normed[:, pl.ds(pl.multiple_of(o * depth, depth), depth)] for o in owners]


def weight_tile(place, pieces, step, matrix):
    share = 4 // len(pieces)
    turn = lax.rem(place[2] - matrix // share + len(pieces), len(pieces))
    chosen = pieces[0][step - 1, matrix % share]
    for t in range(1, len(pieces)):
        chosen = jnp.where(turn == t, pieces[t][step - 1, matrix % share], chosen)
    return chosen


def projected(place, parts, w_own, pieces, matrix):
    terms = [nn(parts[0], w_own[1 + matrix])]
    terms += [
        nn(parts[step], weight_tile(place, pieces, step, matrix)) for step in range(1, len(parts))
    ]
    return functools.reduce(jnp.add, terms)


def store_lse(out, columns):
    length = out.shape[0]
    lanes = lax.broadcasted_iota(jnp.int32, (length, 128), 1)
    table = jnp.zeros((length, 128), F32)
    for head, column in enumerate(columns):
        table = jnp.where(lanes == head, column, table)
    out[...] = table


def local_kernel(
    place,
    decay,
    rate,
    normed,
    query,
    persist,
    memory_in,
    w_own,
    *refs,
    length,
    heads,
):
    pieces = refs[:-7]
    attended, lse_out, recalled, memory_out, keys, values, memory = refs[-7:]
    parts = feature_parts(place, normed, pieces[0].shape[0] + 1, w_own.shape[1])
    keys[...] = projected(place, parts, w_own, pieces, 0).astype(BF16)
    values[...] = projected(place, parts, w_own, pieces, 1).astype(BF16)
    rows = 256
    columns_lse = []
    for head in range(heads):
        lanes = slice(head * HD, (head + 1) * HD)
        pieces = []
        for part in range(length // rows):
            rs = slice(part * rows, (part + 1) * rows)
            span = (part + 1) * rows
            scores = nt(query[rs, lanes], keys[:span, lanes])
            own = part * rows + lax.broadcasted_iota(jnp.int32, (rows, span), 0)
            theirs = lax.broadcasted_iota(jnp.int32, (rows, span), 1)
            scores = jnp.where(own >= theirs, scores, EMPTY)
            fixed = nt(query[rs, lanes], persist[0, :, lanes])
            top = jnp.maximum(
                jnp.max(scores, axis=1, keepdims=True), jnp.max(fixed, axis=1, keepdims=True)
            )
            probs = jnp.exp2((scores - top) * SCALE)
            fixed_probs = jnp.exp2((fixed - top) * SCALE)
            total = jnp.sum(probs, axis=1, keepdims=True) + jnp.sum(
                fixed_probs, axis=1, keepdims=True
            )
            mixed = nn(probs.astype(BF16), values[:span, lanes]) + nn(
                fixed_probs.astype(BF16), persist[1, :, lanes]
            )
            attended[rs, lanes] = mixed / total
            pieces.append(top * SCALE + jnp.log2(total))
        columns_lse.append(jnp.concatenate(pieces, axis=0))
    store_lse(lse_out, columns_lse)

    memory[...] = memory_in[0]

    def update(segment, carry):
        rs = pl.ds(pl.multiple_of(segment * SEG, SEG), SEG)
        for head in range(heads):
            lanes = slice(head * HD, (head + 1) * HD)
            seg_query = query[rs, lanes].astype(F32)
            seg_keys = keys[rs, lanes].astype(F32)
            seg_query = seg_query * lax.rsqrt(
                jnp.sum(seg_query * seg_query, axis=1, keepdims=True) + 1e-06
            )
            seg_keys = seg_keys * lax.rsqrt(
                jnp.sum(seg_keys * seg_keys, axis=1, keepdims=True) + 1e-06
            )
            state = memory[head]
            both = hp(jnp.concatenate([seg_query, seg_keys], axis=0), state, ((1,), (0,)))
            recalled[rs, lanes] = both[:SEG]
            errors = both[SEG:] - values[rs, lanes].astype(F32)
            change = hp(seg_keys, errors, ((0,), (0,)))
            memory[head] = decay[0, segment, head] * state - rate[0, segment, head] * change
        return carry

    lax.fori_loop(0, length // SEG, update, 0, unroll=True)
    memory_out[0] = memory[...]


def local_part(place, decay, rate, normed, query, persist, memory, w_own, pieces):
    length, width = query.shape
    heads = width // HD
    kernel = functools.partial(local_kernel, length=length, heads=heads)
    return pl.pallas_call(
        kernel,
        out_shape=(
            jax.ShapeDtypeStruct((length, width), F32),
            jax.ShapeDtypeStruct((length, 128), F32),
            jax.ShapeDtypeStruct((length, width), F32),
            jax.ShapeDtypeStruct(memory.shape, F32),
        ),
        in_specs=[smem()] * 3 + [vmem()] * (5 + len(pieces)),
        out_specs=(vmem(),) * 4,
        scratch_shapes=[
            pltpu.VMEM((length, width), BF16),
            pltpu.VMEM((length, width), BF16),
            pltpu.VMEM((heads, HD, HD), F32),
        ],
        compiler_params=params(),
        cost_estimate=cost(),
        name="local_part",
    )(place, decay, rate, normed, query, persist, memory, w_own, *pieces)


def early_kernel(
    place, normed, w_own, recalled, attended, lse_in, *refs, count, length, width
):
    pieces, ins = refs[:count], refs[count:-3]
    mixed_out, lse_out, gated = refs[-3:]
    heads = width // HD
    parts = feature_parts(place, normed, pieces[0].shape[0] + 1, w_own.shape[1])
    gated[...] = jax.nn.sigmoid(projected(place, parts, w_own, pieces, 2)) * recalled[...]
    stats = [read_stats(ref, length, width, heads) for ref in ins]
    columns = []
    for head in range(heads):
        lanes = slice(head * HD, (head + 1) * HD)
        mixed, lse = merge(
            [attended[:, lanes]] + [ref[:length, lanes].astype(F32) for ref in ins],
            [lse_in[:, head : head + 1]] + [stat[head] for stat in stats],
        )
        mixed_out[:, lanes] = mixed
        columns.append(lse)
    store_lse(lse_out, columns)


def early_part(place, normed, w_own, pieces, recalled, attended, lse, parts):
    length, width = attended.shape
    kernel = functools.partial(early_kernel, count=len(pieces), length=length, width=width)
    full = jax.ShapeDtypeStruct((length, width), F32)
    return pl.pallas_call(
        kernel,
        out_shape=(full, jax.ShapeDtypeStruct(lse.shape, F32), full),
        in_specs=[smem()] + [vmem()] * (5 + len(pieces) + len(parts)),
        out_specs=(vmem(),) * 3,
        compiler_params=params(),
        cost_estimate=cost(),
        name="early_part",
    )(place, normed, w_own, recalled, attended, lse, *pieces, *parts)


def final_kernel(place, attended, lse_in, gated, w_own, *refs, sources, length, width):
    pieces, ins = refs[:sources], refs[sources:-3]
    send, keep, combined = refs[-3:]
    heads = width // HD
    count = pieces[0].shape[0] + 1
    stats = [read_stats(ref, length, width, heads) for ref in ins]
    for head in range(heads):
        lanes = slice(head * HD, (head + 1) * HD)
        mixed, _ = merge(
            [attended[:, lanes]] + [ref[:length, lanes].astype(F32) for ref in ins],
            [lse_in[:, head : head + 1]] + [s[head] for s in stats],
        )
        combined[:, lanes] = (mixed + gated[:, lanes]).astype(BF16)
    for step in range(count):
        owner = lax.rem(place[0] - step + count, count)
        weights = w_own[4] if step == 0 else weight_tile(place, pieces, step, 3)
        term = nt(combined[...], weights).astype(BF16)
        other = lax.rem(owner + place[1], 2)
        where = lax.div(owner, 2)

        @pl.when(other == 1)
        def _():
            send[where] = term

        @pl.when(other == 0)
        def _():
            keep[where] = term


def final_part(place, attended, lse, gated, parts, w_own, pieces):
    length, width = attended.shape
    kernel = functools.partial(final_kernel, sources=len(pieces), length=length, width=width)
    count = pieces[0].shape[0] + 1
    half = jax.ShapeDtypeStruct((count // 2, length, w_own.shape[1]), BF16)
    return pl.pallas_call(
        kernel,
        out_shape=(half, half),
        in_specs=[smem()] + [vmem()] * (4 + len(pieces) + len(parts)),
        out_specs=(vmem(), vmem()),
        scratch_shapes=[pltpu.VMEM((length, width), BF16)],
        compiler_params=params(),
        cost_estimate=cost(),
        name="final_part",
    )(place, attended, lse, gated, w_own, *pieces, *parts)


def shards(tokens, norm_gain, w_attn, persist_kv, kv_pool, cache_len, mem_state, decay, rate):
    req, row, col = lax.axis_size("req"), lax.axis_size("row"), lax.axis_size("col")
    pool_size = req * row
    my_req, my_row, my_col = lax.axis_index("req"), lax.axis_index("row"), lax.axis_index("col")
    my_index = my_req * row + my_row
    length = tokens.shape[0]
    width = w_attn.shape[2]
    slots, page = kv_pool.shape[2], kv_pool.shape[3]

    def shift(x, axis, by, name):
        size = lax.axis_size(axis)
        with jax.named_scope(name):
            return lax.ppermute(x, axis, [(i, (i + by) % size) for i in range(size)])

    def after(x, *others):
        return lax.optimization_barrier((x,) + others)[0]

    w_query = w_attn[0]
    query_shards = [w_query] + [
        shift(w_query, "row", s, f"query_weights_{s}") for s in range(1, row)
    ]
    xfloat = tokens.astype(F32)
    normed = (
        xfloat * lax.rsqrt(jnp.mean(xfloat * xfloat, axis=-1, keepdims=True) + 1e-05) * norm_gain
    ).astype(BF16)
    groups = min(req, 4)
    group = my_req % groups
    place = jnp.stack([my_row, my_col, group]).astype(jnp.int32)

    numbers = jnp.arange(pool_size, dtype=jnp.int32)
    blocks = ((my_req - numbers % req) % req) * row + (my_row - numbers // req) % row
    offsets = (my_index - blocks) % pool_size
    limits = cache_len[blocks]
    used = jnp.clip(
        ((limits + page - 1) // page - offsets + pool_size - 1) // pool_size, 0, slots
    )
    last = (used - 1) * pool_size + offsets
    info = jnp.stack([blocks, used, limits - last * page], axis=1).astype(jnp.int32)

    cache = lay_out_pages(kv_pool[0].reshape(pool_size, slots * page, 2, width))
    normed, info, place = lax.optimization_barrier((normed, info, place, cache))[:3]
    queries = project(place, normed, query_shards)

    order = list(dict.fromkeys([s for s in (1, row - 1) if 0 < s < row] + list(range(1, row))))
    final_step = order[-1]
    previous = [info]
    partials, back = {}, {}

    def attend(s, t, here, *first):
        info_now = after(info, previous[0], *first)
        previous[0] = partials[s, t] = pool_attend(
            s * req + t, info_now, here, cache, slots, page
        )

    def send_back(s, *first):
        back[s] = [
            shift(after(partials[s, t], *first), "req", -t, f"partials_req_{s}")
            for t in range(1, req)
        ]

    def over_row(x, name):
        got = {s: shift(x, "row", s, f"{name}_row_{s}") for s in order if s in (1, row - 1)}
        for s in range(2, row - 1):
            got[s] = shift(got[s - 1], "row", 1, f"{name}_row_{s}")
        return got

    by_row = over_row(queries, "queries")
    there = [shift(queries, "req", t, "queries_req_0") for t in range(1, req)]
    attend(0, 0, queries)
    for t in range(1, req):
        attend(0, t, there[t - 1])

    share = 4 // groups
    w_share = lax.dynamic_slice_in_dim(w_attn, 1 + group * share, share, 0)
    near = [by_row[s] for s in order if s in (1, row - 1)]
    fetched = over_row(after(w_share, *near), "weights")

    for s in order:
        moved = after(by_row[s], previous[0])
        there = [shift(moved, "req", t, f"queries_req_{s}") for t in range(1, req)]
        attend(s, 0, by_row[s])
        if s == final_step:
            previous.append(fetched[order[0]])
        for t in range(1, req):
            attend(s, t, there[t - 1], *previous[1:])
        if s == final_step:
            send_back(s, *[part for done in order[:-1] for part in back[done]])
        else:
            send_back(s)
    fetched = jnp.stack([fetched[s] for s in range(1, row)])
    arrived = {}
    for s in order:
        parts = [partials[s, 0]] + back[s]
        if s == final_step:
            parts[0] = after(parts[0], fetched)
        arrived[s] = merge_parts(parts, length, width)
    merged_last = arrived[final_step]
    for s in order:
        arrived[s] = shift(arrived[s], "row", -s, f"partials_row_{s}")
    moved = after(fetched, *back[final_step])
    pieces = [fetched] + [shift(moved, "req", t, "weights_req") for t in range(1, groups)]
    send_back(0, *back[final_step])

    local_out, local_lse, recalled, new_state = local_part(
        place,
        decay,
        rate,
        normed,
        after(queries, merged_last),
        persist_kv,
        mem_state,
        w_attn,
        pieces,
    )
    early = [partials[0, 0]] + back[0] + [arrived[s] for s in order[:-1]]
    mixed, lse, gated = early_part(
        place, normed, w_attn, pieces, recalled, local_out, local_lse, early
    )
    send, keep = final_part(place, mixed, lse, gated, [arrived[final_step]], w_attn, pieces)
    with jax.named_scope("output_pairs"):
        got = lax.ppermute(send, "col", [(i, i ^ 1) for i in range(col)])
    summed = keep.astype(F32) + got.astype(F32)
    spot = my_col // 2
    own = lax.dynamic_index_in_dim(summed, spot, 0, keepdims=False)
    mine = lax.dynamic_slice_in_dim(xfloat, my_col * own.shape[1], own.shape[1], 1) + own
    for step in range(1, col // 2):
        away = lax.dynamic_index_in_dim(summed, spot ^ step, 0, keepdims=False).astype(BF16)
        with jax.named_scope("output_quarters"):
            came = lax.ppermute(away, "col", [(i, i ^ (2 * step)) for i in range(col)])
        mine = mine + came.astype(F32)
    return (mine.astype(BF16), new_state)


def solution(mesh):
    return jax.shard_map(
        shards,
        mesh=mesh,
        in_specs=(
            P(("req", "row"), None),
            P(),
            P(None, "row", "col"),
            P(None, None, "col"),
            P(("req", "row"), None, None, None, None, "col"),
            P(),
            P(("req", "row"), "col", None, None),
            P(("req", "row"), None, "col"),
            P(("req", "row"), None, "col"),
        ),
        out_specs=(P(("req", "row"), "col"), P(("req", "row"), "col", None, None)),
        check_vma=False,
    )
```

```python
import functools

import jax
import jax.numpy as jnp
from jax import lax
from jax.experimental import pallas as pl
from jax.experimental.pallas import tpu as pltpu
from jax.sharding import PartitionSpec as P

HD = 128
NP = 16
SEG = 64
LOG2E = 1.4426950408889634
SCALE = HD ** (-0.5) * LOG2E
EMPTY = -1e30
STAT = 16
F32 = jnp.float32
BF16 = jnp.bfloat16
VMEM_LIMIT = 16 * 1024 * 1024
LOAD_LIMIT = 52 * 1024 * 1024


def nt(a, b):
    return lax.dot_general(a, b, (((1,), (1,)), ((), ())), preferred_element_type=F32)


def nn(a, b):
    return lax.dot_general(a, b, (((1,), (0,)), ((), ())), preferred_element_type=F32)


def split3(x):
    high = x.astype(BF16).astype(F32)
    rest = x - high
    middle = rest.astype(BF16).astype(F32)
    return high, middle, (rest - middle).astype(BF16).astype(F32)


def write_stats(out_ref, length, width, lse):
    lanes = lax.broadcasted_iota(jnp.int32, (length, 128), 1)
    table = jnp.zeros((length, 128), F32)
    place = 0
    for column in lse:
        for piece in split3(column):
            table = jnp.where(lanes == place, piece, table)
            place += 1
    rows = jnp.transpose(table)[:8]
    parts = length // width
    packed = jnp.concatenate(
        [rows[:, part * width : (part + 1) * width] for part in range(parts)], axis=0
    )
    out_ref[length : length + 8 * parts, :] = packed.astype(BF16)


def read_stats(ref, length, width, heads):
    parts = length // width
    packed = ref[length : length + 8 * parts, :].astype(F32)
    rows = jnp.concatenate([packed[8 * part : 8 * part + 8] for part in range(parts)], axis=1)
    rows = jnp.concatenate([rows, jnp.zeros((120, length), F32)], axis=0)
    table = jnp.transpose(rows)
    return [
        table[:, 3 * head : 3 * head + 1]
        + table[:, 3 * head + 1 : 3 * head + 2]
        + table[:, 3 * head + 2 : 3 * head + 3]
        for head in range(heads)
    ]


def project_kernel(place, normed, *refs):
    shards, out = refs[:-1], refs[-1]
    depth = shards[0].shape[0]
    count = len(shards)
    total = None
    for step in range(count):
        owner = lax.rem(place[0] - step + count, count)
        part = normed[:, pl.ds(pl.multiple_of(owner * depth, depth), depth)]
        term = nn(part, shards[step][...])
        total = term if total is None else total + term
    out[...] = total.astype(BF16)


def smem():
    return pl.BlockSpec(memory_space=pltpu.SMEM)


def vmem():
    return pl.BlockSpec(memory_space=pltpu.VMEM)


def params(limit=VMEM_LIMIT):
    return pltpu.CompilerParams(vmem_limit_bytes=limit)


OPT = dict(
    c=0.3, kchain=1, korder=4, ytie=2, wtie="far", wytie=0, mtie=0, loc=0, relayq=1, relayw=1,
    p0=0, lay=2, ptie=0, rtie=2, fuse=2, morder=0, groups=0,
)


def cost(microseconds):
    size = max(1, int(3e6 * OPT["c"] * microseconds))
    return pl.CostEstimate(flops=1, bytes_accessed=size, transcendentals=0)


def project(place, normed, shards):
    length, width = normed.shape[0], shards[0].shape[1]
    return pl.pallas_call(
        project_kernel,
        out_shape=jax.ShapeDtypeStruct((length, width), BF16),
        in_specs=[smem()] + [vmem()] * (1 + len(shards)),
        out_specs=vmem(),
        compiler_params=params(),
        cost_estimate=cost(1),
        name="project_queries",
    )(place, normed, *shards)


def load_kernel(info, pages, *refs, slots, page):
    outs, sems = refs[:-1], refs[-1]
    tiles = [(k, slot) for k in range(len(outs)) for slot in range(slots)]

    def fetch(k, slot):
        rows = pl.ds(slot * page, page)
        return pltpu.make_async_copy(
            pages.at[info[k, 0], rows], outs[k].at[rows], sems.at[k, slot]
        )

    for k, slot in tiles:
        pl.when(slot < info[k, 1])(lambda k=k, slot=slot: fetch(k, slot).start())
    for k, slot in tiles:
        pl.when(slot < info[k, 1])(lambda k=k, slot=slot: fetch(k, slot).wait())


def load_pages(info, pages, slots):
    blocks, span, _, width = pages.shape
    kernel = functools.partial(load_kernel, slots=slots, page=span // slots)
    return pl.pallas_call(
        kernel,
        out_shape=(jax.ShapeDtypeStruct((span, 2, width), BF16),) * blocks,
        in_specs=[smem(), pl.BlockSpec(memory_space=pltpu.HBM)],
        out_specs=(vmem(),) * blocks,
        scratch_shapes=[pltpu.SemaphoreType.DMA((blocks, slots))],
        compiler_params=params(LOAD_LIMIT),
        cost_estimate=cost(4),
        name="load_pages",
    )(info, pages)


def pool_kernel(info, query, pages, *refs, which, slots, page, heads, length, width):
    ins = refs[:-4]
    out, cache, own, own_lse = refs[-4:]
    used, remain = info[which, 1], info[which, 2]
    lanes_at = lax.broadcasted_iota(jnp.int32, (length, 128), 1)

    @pl.when(used == 0)
    def _():
        own[...] = jnp.zeros(own.shape, F32)
        own_lse[...] = jnp.full(own_lse.shape, EMPTY, F32)

    for count in range(1, slots + 1):

        @pl.when(used == count)
        def _(count=count):
            span = count * page
            cache[:span] = pages[:span].reshape(span, 2 * width)
            columns = lax.broadcasted_iota(jnp.int32, (length, page), 1)
            table = jnp.zeros((length, 128), F32)
            for head in range(heads):
                lanes = slice(head * HD, (head + 1) * HD)
                after = slice(width + head * HD, width + (head + 1) * HD)
                scores = nt(query[:, lanes], cache[:span, lanes])
                last = jnp.where(columns < remain, scores[:, span - page :], EMPTY)
                if count > 1:
                    scores = jnp.concatenate([scores[:, : span - page], last], axis=1)
                else:
                    scores = last
                top = jnp.max(scores, axis=1, keepdims=True)
                probs = jnp.exp2((scores - top) * SCALE)
                total = jnp.sum(probs, axis=1, keepdims=True)
                mixed = nn(probs.astype(BF16), cache[:span, after])
                own[:, lanes] = mixed / total
                table = jnp.where(lanes_at == head, top * SCALE + jnp.log2(total), table)
            own_lse[...] = table

    stats = [read_stats(ref, length, width, heads) for ref in ins]
    lse = []
    for head in range(heads):
        lanes = slice(head * HD, (head + 1) * HD)
        mixed, head_lse = own[:, lanes], own_lse[:, head : head + 1]
        if ins:
            mixed, head_lse = merge(
                [mixed] + [ref[:length, lanes].astype(F32) for ref in ins],
                [head_lse] + [stat[head] for stat in stats],
            )
        out[:length, lanes] = mixed.astype(BF16)
        lse.append(head_lse)
    write_stats(out, length, width, lse)


def pool_attend(which, info, query, pages, parts, slots, page):
    length, width = query.shape
    span = slots * page
    kernel = functools.partial(
        pool_kernel,
        which=which,
        slots=slots,
        page=page,
        heads=width // HD,
        length=length,
        width=width,
    )
    return pl.pallas_call(
        kernel,
        out_shape=jax.ShapeDtypeStruct((length + STAT, width), BF16),
        in_specs=[smem()] + [vmem()] * (2 + len(parts)),
        out_specs=vmem(),
        scratch_shapes=[
            pltpu.VMEM((span, 2 * width), BF16),
            pltpu.VMEM((length, width), F32),
            pltpu.VMEM((length, 128), F32),
        ],
        compiler_params=params(),
        cost_estimate=cost(3),
        name="pool_attention",
    )(info, query, pages, *parts)


def merge(parts, lse):
    top = functools.reduce(jnp.maximum, lse)
    weights = [jnp.exp2(one - top) for one in lse]
    total = functools.reduce(jnp.add, weights)
    mixed = functools.reduce(jnp.add, [w * p for w, p in zip(weights, parts)])
    return mixed / total, top + jnp.log2(total)


def merge_kernel(*refs, length, width, heads):
    ins, out = refs[:-1], refs[-1]
    stats = [read_stats(ref, length, width, heads) for ref in ins]
    merged = []
    for head in range(heads):
        lanes = slice(head * HD, (head + 1) * HD)
        mixed, lse = merge(
            [ref[:length, lanes].astype(F32) for ref in ins], [s[head] for s in stats]
        )
        out[:length, lanes] = mixed.astype(BF16)
        merged.append(lse)
    write_stats(out, length, width, merged)


def merge_parts(parts, length, width):
    kernel = functools.partial(merge_kernel, length=length, width=width, heads=width // HD)
    return pl.pallas_call(
        kernel,
        out_shape=jax.ShapeDtypeStruct((length + STAT, width), BF16),
        in_specs=[vmem()] * len(parts),
        out_specs=vmem(),
        compiler_params=params(),
        cost_estimate=cost(2),
        name="merge_partials",
    )(*parts)


def hp(a, b, dims):
    def halves(x):
        high = x.astype(BF16)
        return high, (x - high.astype(F32)).astype(BF16)

    def dot(x, y):
        return lax.dot_general(x, y, (dims, ((), ())), preferred_element_type=F32)

    a_high, a_low = halves(a)
    b_high, b_low = halves(b)
    return dot(a_high, b_high) + (dot(a_high, b_low) + dot(a_low, b_high))


def feature_parts(place, normed, count, depth):
    owners = [lax.rem(place[0] - step + count, count) for step in range(count)]
    return [normed[:, pl.ds(pl.multiple_of(o * depth, depth), depth)] for o in owners]


def weight_tile(place, pieces, step, matrix):
    here = pieces[step - 1]
    share = 4 // len(here)
    turn = lax.rem(place[2] - matrix // share + len(here), len(here))
    chosen = here[0][matrix % share]
    for t in range(1, len(here)):
        chosen = jnp.where(turn == t, here[t][matrix % share], chosen)
    return chosen


def regroup(refs, row):
    groups = len(refs) // (row - 1)
    return [refs[i * groups : (i + 1) * groups] for i in range(row - 1)]


def projected(place, parts, w_own, pieces, matrix):
    terms = [nn(parts[0], w_own[1 + matrix])]
    terms += [
        nn(parts[step], weight_tile(place, pieces, step, matrix)) for step in range(1, len(parts))
    ]
    return functools.reduce(jnp.add, terms)


def store_lse(out, columns):
    length = out.shape[0]
    lanes = lax.broadcasted_iota(jnp.int32, (length, 128), 1)
    table = jnp.zeros((length, 128), F32)
    for head, column in enumerate(columns):
        table = jnp.where(lanes == head, column, table)
    out[...] = table


def local_kernel(
    place,
    decay,
    rate,
    normed,
    query,
    persist,
    memory_in,
    w_own,
    *refs,
    row,
    length,
    heads,
):
    pieces = regroup(refs[:-7], row)
    attended, lse_out, recalled, memory_out, keys, values, memory = refs[-7:]
    parts = feature_parts(place, normed, row, w_own.shape[1])
    keys[...] = projected(place, parts, w_own, pieces, 0).astype(BF16)
    values[...] = projected(place, parts, w_own, pieces, 1).astype(BF16)
    rows = 256
    columns_lse = []
    for head in range(heads):
        lanes = slice(head * HD, (head + 1) * HD)
        pieces = []
        for part in range(length // rows):
            rs = slice(part * rows, (part + 1) * rows)
            span = (part + 1) * rows
            scores = nt(query[rs, lanes], keys[:span, lanes])
            own = part * rows + lax.broadcasted_iota(jnp.int32, (rows, span), 0)
            theirs = lax.broadcasted_iota(jnp.int32, (rows, span), 1)
            scores = jnp.where(own >= theirs, scores, EMPTY)
            fixed = nt(query[rs, lanes], persist[0, :, lanes])
            top = jnp.maximum(
                jnp.max(scores, axis=1, keepdims=True), jnp.max(fixed, axis=1, keepdims=True)
            )
            probs = jnp.exp2((scores - top) * SCALE)
            fixed_probs = jnp.exp2((fixed - top) * SCALE)
            total = jnp.sum(probs, axis=1, keepdims=True) + jnp.sum(
                fixed_probs, axis=1, keepdims=True
            )
            mixed = nn(probs.astype(BF16), values[:span, lanes]) + nn(
                fixed_probs.astype(BF16), persist[1, :, lanes]
            )
            attended[rs, lanes] = mixed / total
            pieces.append(top * SCALE + jnp.log2(total))
        columns_lse.append(jnp.concatenate(pieces, axis=0))
    store_lse(lse_out, columns_lse)

    memory[...] = memory_in[0]

    def update(segment, carry):
        rs = pl.ds(pl.multiple_of(segment * SEG, SEG), SEG)
        for head in range(heads):
            lanes = slice(head * HD, (head + 1) * HD)
            seg_query = query[rs, lanes].astype(F32)
            seg_keys = keys[rs, lanes].astype(F32)
            seg_query = seg_query * lax.rsqrt(
                jnp.sum(seg_query * seg_query, axis=1, keepdims=True) + 1e-06
            )
            seg_keys = seg_keys * lax.rsqrt(
                jnp.sum(seg_keys * seg_keys, axis=1, keepdims=True) + 1e-06
            )
            state = memory[head]
            both = hp(jnp.concatenate([seg_query, seg_keys], axis=0), state, ((1,), (0,)))
            recalled[rs, lanes] = both[:SEG]
            errors = both[SEG:] - values[rs, lanes].astype(F32)
            change = hp(seg_keys, errors, ((0,), (0,)))
            memory[head] = decay[0, segment, head] * state - rate[0, segment, head] * change
        return carry

    lax.fori_loop(0, length // SEG, update, 0, unroll=True)
    memory_out[0] = memory[...]


def local_part(place, decay, rate, normed, query, persist, memory, w_own, pieces, row):
    length, width = query.shape
    heads = width // HD
    kernel = functools.partial(local_kernel, row=row, length=length, heads=heads)
    return pl.pallas_call(
        kernel,
        out_shape=(
            jax.ShapeDtypeStruct((length, width), F32),
            jax.ShapeDtypeStruct((length, 128), F32),
            jax.ShapeDtypeStruct((length, width), F32),
            jax.ShapeDtypeStruct(memory.shape, F32),
        ),
        in_specs=[smem()] * 3 + [vmem()] * (5 + len(pieces)),
        out_specs=(vmem(),) * 4,
        scratch_shapes=[
            pltpu.VMEM((length, width), BF16),
            pltpu.VMEM((length, width), BF16),
            pltpu.VMEM((heads, HD, HD), F32),
        ],
        compiler_params=params(),
        cost_estimate=cost(6),
        name="local_part",
    )(place, decay, rate, normed, query, persist, memory, w_own, *pieces)


def early_kernel(
    place, normed, w_own, recalled, attended, lse_in, *refs, count, row, length, width
):
    pieces, ins = regroup(refs[:count], row), refs[count:-3]
    mixed_out, lse_out, gated = refs[-3:]
    heads = width // HD
    parts = feature_parts(place, normed, row, w_own.shape[1])
    gated[...] = jax.nn.sigmoid(projected(place, parts, w_own, pieces, 2)) * recalled[...]
    stats = [read_stats(ref, length, width, heads) for ref in ins]
    columns = []
    for head in range(heads):
        lanes = slice(head * HD, (head + 1) * HD)
        mixed, lse = merge(
            [attended[:, lanes]] + [ref[:length, lanes].astype(F32) for ref in ins],
            [lse_in[:, head : head + 1]] + [stat[head] for stat in stats],
        )
        mixed_out[:, lanes] = mixed
        columns.append(lse)
    store_lse(lse_out, columns)


def early_part(place, normed, w_own, pieces, row, recalled, attended, lse, parts):
    length, width = attended.shape
    kernel = functools.partial(
        early_kernel, count=len(pieces), row=row, length=length, width=width
    )
    full = jax.ShapeDtypeStruct((length, width), F32)
    return pl.pallas_call(
        kernel,
        out_shape=(full, jax.ShapeDtypeStruct(lse.shape, F32), full),
        in_specs=[smem()] + [vmem()] * (5 + len(pieces) + len(parts)),
        out_specs=(vmem(),) * 3,
        compiler_params=params(),
        cost_estimate=cost(4),
        name="early_part",
    )(place, normed, w_own, recalled, attended, lse, *pieces, *parts)


def final_kernel(place, attended, lse_in, gated, w_own, *refs, sources, row, length, width):
    pieces, ins = regroup(refs[:sources], row), refs[sources:-3]
    send, keep, combined = refs[-3:]
    heads = width // HD
    count = row
    stats = [read_stats(ref, length, width, heads) for ref in ins]
    for head in range(heads):
        lanes = slice(head * HD, (head + 1) * HD)
        mixed, _ = merge(
            [attended[:, lanes]] + [ref[:length, lanes].astype(F32) for ref in ins],
            [lse_in[:, head : head + 1]] + [s[head] for s in stats],
        )
        combined[:, lanes] = (mixed + gated[:, lanes]).astype(BF16)
    for step in range(count):
        owner = lax.rem(place[0] - step + count, count)
        weights = w_own[4] if step == 0 else weight_tile(place, pieces, step, 3)
        term = nt(combined[...], weights).astype(BF16)
        other = lax.rem(owner + place[1], 2)
        where = lax.div(owner, 2)

        @pl.when(other == 1)
        def _():
            send[where] = term

        @pl.when(other == 0)
        def _():
            keep[where] = term


def final_part(place, attended, lse, gated, parts, w_own, pieces, row):
    length, width = attended.shape
    kernel = functools.partial(
        final_kernel, sources=len(pieces), row=row, length=length, width=width
    )
    count = row
    half = jax.ShapeDtypeStruct((count // 2, length, w_own.shape[1]), BF16)
    return pl.pallas_call(
        kernel,
        out_shape=(half, half),
        in_specs=[smem()] + [vmem()] * (4 + len(pieces) + len(parts)),
        out_specs=(vmem(), vmem()),
        scratch_shapes=[pltpu.VMEM((length, width), BF16)],
        compiler_params=params(),
        cost_estimate=cost(3),
        name="final_part",
    )(place, attended, lse, gated, w_own, *pieces, *parts)


def pair_kernel(place, tokens, keep, got, mine, away):
    spot = lax.div(place[1], 2)
    mine[...] = tokens[...].astype(F32) + (keep[spot].astype(F32) + got[spot].astype(F32))
    for step in range(1, keep.shape[0]):
        other = jnp.bitwise_xor(spot, step)
        away[step - 1] = (keep[other].astype(F32) + got[other].astype(F32)).astype(BF16)


def pair_sum(place, tokens, keep, got):
    count, length, width = keep.shape
    return pl.pallas_call(
        pair_kernel,
        out_shape=(
            jax.ShapeDtypeStruct((length, width), F32),
            jax.ShapeDtypeStruct((count - 1, length, width), BF16),
        ),
        in_specs=[smem()] + [vmem()] * 3,
        out_specs=(vmem(), vmem()),
        compiler_params=params(),
        cost_estimate=cost(1),
        name="pair_sum",
    )(place, tokens, keep, got)


def shards(tokens, norm_gain, w_attn, persist_kv, kv_pool, cache_len, mem_state, decay, rate):
    req, row, col = lax.axis_size("req"), lax.axis_size("row"), lax.axis_size("col")
    pool_size = req * row
    my_req, my_row, my_col = lax.axis_index("req"), lax.axis_index("row"), lax.axis_index("col")
    my_index = my_req * row + my_row
    length = tokens.shape[0]
    width = w_attn.shape[2]
    slots, page = kv_pool.shape[2], kv_pool.shape[3]

    def shift(x, axis, by, name):
        size = lax.axis_size(axis)
        with jax.named_scope(name):
            return lax.ppermute(x, axis, [(i, (i + by) % size) for i in range(size)])

    def after(x, *others):
        return lax.optimization_barrier((x,) + others)[0]

    w_query = w_attn[0]
    query_shards = [w_query] + [
        shift(w_query, "row", s, f"query_weights_{s}") for s in range(1, row)
    ]
    xfloat = tokens.astype(F32)
    normed = (
        xfloat * lax.rsqrt(jnp.mean(xfloat * xfloat, axis=-1, keepdims=True) + 1e-05) * norm_gain
    ).astype(BF16)
    groups = min(req, 4) if OPT["groups"] else 1
    group = my_req % groups
    place = jnp.stack([my_row, my_col, group]).astype(jnp.int32)

    order = [0] + list(dict.fromkeys([s for s in (1, row - 1) if 0 < s < row] + list(range(1, row))))
    steps = jnp.asarray(order, jnp.int32)[:, None]
    turns = jnp.arange(req, dtype=jnp.int32)[None, :]
    blocks = (((my_req - turns) % req) * row + (my_row - steps) % row).reshape(-1)
    offsets = (my_index - blocks) % pool_size
    limits = cache_len[blocks]
    used = jnp.clip(
        ((limits + page - 1) // page - offsets + pool_size - 1) // pool_size, 0, slots
    )
    last = (used - 1) * pool_size + offsets
    info = jnp.stack([blocks, used, limits - last * page], axis=1).astype(jnp.int32)

    pages = kv_pool[0].reshape(pool_size, slots * page, 2, width)
    if OPT["lay"] == 1:
        pages = load_pages(info, pages, slots)
        place = after(place, *pages)
    queries = project(place, normed, query_shards)
    if OPT["lay"] == 2:
        pages = load_pages(after(info, queries), pages, slots)

    order = order[1:]
    far = order[-1]
    numbered = {}
    for s in [0] + order:
        for t in range(req):
            numbered[s, t] = len(numbered)
    partials, back, arrived = {}, {}, {}
    latest = [queries]
    outs = []

    def attend(s, t, here, parts=()):
        number = numbered[s, t]
        info_now = after(info, latest[0]) if OPT["kchain"] else info
        latest[0] = partials[s, t] = pool_attend(
            number, info_now, here, pages[number], parts, slots, page
        )
        outs.append(latest[0])

    def send_back(s, *first):
        back[s] = [
            shift(after(partials[s, t], *first), "req", -t, f"partials_req_{s}")
            for t in range(1, req)
        ]

    def merge_arrived(s, *first):
        if (s, 0) not in partials:
            attend(s, 0, after(by_row[s], *first), back[s])
            arrived[s] = latest[0]
            return
        if OPT["kchain"]:
            first = (latest[0],) + first
        parts = [after(partials[s, 0], *first)] + back[s]
        latest[0] = arrived[s] = merge_parts(parts, length, width)

    def over_row(x, name, relay, *first):
        got = {}
        for s in order:
            if s in (1, row - 1) or not relay:
                got[s] = shift(x, "row", s, f"{name}_row_{s}")
            else:
                moved = after(got[s - 1], *first)
                got[s] = shift(moved, "row", 1, f"{name}_row_{s}")
        return got

    def over_req(x, name, *first):
        return [shift(after(x, *first), "req", t, name) for t in range(1, req)]

    by_row = over_row(queries, "queries", OPT["relayq"])
    by_row[0] = queries
    there = {0: over_req(queries, "queries_req_0")}
    sequence = [(0, 0)] + [(0, t) for t in range(1, req)]
    if OPT["korder"] == 0:
        for s in order:
            sequence += [(s, t) for t in range(req)]
    elif OPT["korder"] == 1:
        sequence += [(s, 0) for s in order[:-1]]
        sequence += [(s, t) for s in order[:-1] for t in range(1, req)]
        sequence += [(order[-1], t) for t in range(req)]
    elif OPT["korder"] in (4, 5):
        one, near = order[0], order[1:-1]
        sequence = [(0, 0), (one, 0)] + [(0, t) for t in range(1, req)]
        sequence += [(one, t) for t in range(1, req)]
        if OPT["korder"] == 4:
            sequence += [(far, 0)] + [(s, t) for s in near for t in range(req)]
            sequence += [(far, t) for t in range(1, req)]
        else:
            sequence += [(s, 0) for s in near] + [(far, 0)]
            sequence += [(far, t) for t in range(1, req)]
            sequence += [(s, t) for s in near for t in range(1, req)]
    elif OPT["korder"] == 2:
        sequence = [(0, 0)] + [(s, 0) for s in order[:1]] + [(0, t) for t in range(1, req)]
        sequence += [(s, t) for s in order[:1] for t in range(1, req)]
        for s in order[1:]:
            sequence += [(s, t) for t in range(req)]
    else:
        sequence = [(0, 0)] + [(s, 0) for s in order[:1]]
        sequence += [(s, t) for s in order[:1] for t in range(1, req)]
        for s in order[1:]:
            sequence += [(s, t) for t in range(req)]
        sequence += [(0, t) for t in range(1, req)]
    fused = order[len(order) - OPT["fuse"] :]
    sequence = [(s, t) for s, t in sequence if t or s not in fused]
    when = {0: -1}
    for i, s in enumerate(order):
        when[s] = i
    for i, (s, t) in enumerate(sequence):
        if i == 1:
            first = outs if OPT["rtie"] == 1 else pages if OPT["rtie"] == 2 else []
            for f in range(2, row - 1):
                moved = after(by_row[f - 1], *first)
                by_row[f] = shift(moved, "row", 1, f"queries_row_{f}")
        if t and s not in there:
            first = []
            if OPT["ytie"] and when[s] >= 0:
                first = [outs[min(when[s], i - 1)]]
                if OPT["ytie"] == 2:
                    first = [outs[{order[0]: 0, far: 3}.get(s, 1)]]
                if OPT["ytie"] == 3:
                    first = [outs[{order[0]: 0, far: 2}.get(s, 1)]]
            there[s] = over_req(by_row[s], f"queries_req_{s}", *first)
            if OPT["ytie"] > 1 and s == order[0]:
                for other in order[1:-1]:
                    there[other] = over_req(by_row[other], f"queries_req_{other}", outs[1])
        attend(s, t, there[s][t - 1] if t else by_row[s])
    for s in order:
        first = []
        if OPT["ptie"] and s == far:
            first = [part for done in order[:-1] for part in back[done]]
        send_back(s, *first)

    share = 4 // groups
    w_share = lax.dynamic_slice_in_dim(w_attn, 1 + group * share, share, 0)
    ties = dict(
        q=[queries],
        near=[by_row[order[0]]],
        near2=[by_row[s] for s in order[:2]],
        far=[by_row[far]],
        all=[by_row[s] for s in order] + [outs[2]],
        k4=[outs[min(4, len(outs) - 1)]],
    )
    fetched = over_row(after(w_share, *ties[OPT["wtie"]]), "weights", OPT["relayw"])
    pieces = []
    for s in range(1, row):
        moved = fetched[s]
        if OPT["wytie"] == 1:
            moved = after(moved, outs[-1])
        elif OPT["wytie"] == 2:
            moved = after(moved, *back[far])
        elif OPT["wytie"] == 3 and s not in (1, row - 1):
            moved = after(moved, *back[far])
        pieces += [fetched[s]] + [
            shift(moved, "req", t, f"weights_req_{s}") for t in range(1, groups)
        ]
    for s in order if OPT["morder"] == 0 else order[::-1]:
        first = []
        if OPT["mtie"] == 1 and s == order[0]:
            first = [fetched[far]]
        if OPT["mtie"] == 2 and s == far:
            first = [fetched[far]]
        merge_arrived(s, *first)
    merged_last = latest[0]
    for s in order:
        arrived[s] = shift(arrived[s], "row", -s, f"partials_row_{s}")
    send_back(0, *([merged_last] if OPT["p0"] == 1 else [] if OPT["p0"] == 0 else [outs[-1]]))
    if not OPT["loc"]:
        merged_last = queries

    local_out, local_lse, recalled, new_state = local_part(
        place,
        decay,
        rate,
        normed,
        after(queries, merged_last),
        persist_kv,
        mem_state,
        w_attn,
        pieces,
        row,
    )
    early = [partials[0, 0]] + back[0] + [arrived[s] for s in order[:-1]]
    mixed, lse, gated = early_part(
        place, normed, w_attn, pieces, row, recalled, local_out, local_lse, early
    )
    send, keep = final_part(place, mixed, lse, gated, [arrived[far]], w_attn, pieces, row)
    with jax.named_scope("output_pairs"):
        got = lax.ppermute(send, "col", [(i, i ^ 1) for i in range(col)])
    own_cols = lax.dynamic_slice_in_dim(tokens, my_col * keep.shape[2], keep.shape[2], 1)
    mine, away = pair_sum(place, own_cols, keep, got)
    for step in range(1, col // 2):
        with jax.named_scope("output_quarters"):
            came = lax.ppermute(away[step - 1], "col", [(i, i ^ (2 * step)) for i in range(col)])
        mine = mine + came.astype(F32)
    return (mine.astype(BF16), new_state)


def solution(mesh):
    return jax.shard_map(
        shards,
        mesh=mesh,
        in_specs=(
            P(("req", "row"), None),
            P(),
            P(None, "row", "col"),
            P(None, None, "col"),
            P(("req", "row"), None, None, None, None, "col"),
            P(),
            P(("req", "row"), "col", None, None),
            P(("req", "row"), None, "col"),
            P(("req", "row"), None, "col"),
        ),
        out_specs=(P(("req", "row"), "col"), P(("req", "row"), "col", None, None)),
        check_vma=False,
    )
```

```python
import functools

import jax
import jax.numpy as jnp
from jax import lax
from jax.experimental import pallas as pl
from jax.experimental.pallas import tpu as pltpu
from jax.sharding import PartitionSpec as P

HD = 128
NP = 16
SEG = 64
LOG2E = 1.4426950408889634
SCALE = HD ** (-0.5) * LOG2E
EMPTY = -1e30
STAT = 16
F32 = jnp.float32
BF16 = jnp.bfloat16
VMEM_LIMIT = 16 * 1024 * 1024
LOAD_LIMIT = 52 * 1024 * 1024


def nt(a, b):
    return lax.dot_general(a, b, (((1,), (1,)), ((), ())), preferred_element_type=F32)


def nn(a, b):
    return lax.dot_general(a, b, (((1,), (0,)), ((), ())), preferred_element_type=F32)


def split3(x):
    high = x.astype(BF16).astype(F32)
    rest = x - high
    middle = rest.astype(BF16).astype(F32)
    return high, middle, (rest - middle).astype(BF16).astype(F32)


def stack_rows(rows, count=8):
    length = rows[0].shape[1]
    spots = lax.broadcasted_iota(jnp.int32, (count, length), 0)
    table = jnp.zeros((count, length), F32)
    for spot, row in enumerate(rows):
        table = jnp.where(spots == spot, row, table)
    return table


def to_columns(rows):
    length = rows[0].shape[1]
    count = (len(rows) + 7) // 8 * 8
    table = jnp.concatenate(
        [stack_rows(rows, count), jnp.zeros((128 - count, length), F32)], axis=0
    )
    table = jnp.transpose(table)
    return [table[:, spot : spot + 1] for spot in range(len(rows))]


def to_rows(table, heads):
    rows = jnp.transpose(table)[:8]
    return [rows[head : head + 1] for head in range(heads)]


def write_stats(out_ref, length, width, lse):
    rows = stack_rows([piece for row in lse for piece in split3(row)])
    parts = length // width
    packed = jnp.concatenate(
        [rows[:, part * width : (part + 1) * width] for part in range(parts)], axis=0
    )
    out_ref[length : length + 8 * parts, :] = packed.astype(BF16)


def read_stats(ref, length, width, heads):
    parts = length // width
    packed = ref[length : length + 8 * parts, :].astype(F32)
    rows = jnp.concatenate([packed[8 * part : 8 * part + 8] for part in range(parts)], axis=1)
    return [
        rows[3 * head : 3 * head + 1]
        + rows[3 * head + 1 : 3 * head + 2]
        + rows[3 * head + 2 : 3 * head + 3]
        for head in range(heads)
    ]


def merge_weights(stats):
    rows, merged = [], []
    heads = len(stats[0])
    for head in range(heads):
        lse = [stat[head] for stat in stats]
        top = functools.reduce(jnp.maximum, lse)
        weights = [jnp.exp2(one - top) for one in lse]
        total = functools.reduce(jnp.add, weights)
        rows += [weight / total for weight in weights]
        merged.append(top + jnp.log2(total))
    columns = to_columns(rows)
    count = len(stats)
    return [columns[head * count : (head + 1) * count] for head in range(heads)], merged


def project_kernel(place, normed, *refs):
    shards, out = refs[:-1], refs[-1]
    depth = shards[0].shape[0]
    count = len(shards)
    total = None
    for step in range(count):
        owner = lax.rem(place[0] - step + count, count)
        part = normed[:, pl.ds(pl.multiple_of(owner * depth, depth), depth)]
        term = nn(part, shards[step][...])
        total = term if total is None else total + term
    out[...] = total.astype(BF16)


def smem():
    return pl.BlockSpec(memory_space=pltpu.SMEM)


def vmem():
    return pl.BlockSpec(memory_space=pltpu.VMEM)


def params(limit=VMEM_LIMIT):
    return pltpu.CompilerParams(vmem_limit_bytes=limit)


OPT = dict(
    c=0.3, kchain=1, korder=4, ytie=2, wtie="near2", wytie=0, mtie=0, loc=0, relayq=1, relayw=1,
    p0=0, ztie=0, wk=0, lay=2, ptie=0, rtie=2, fuse=2, morder=0, groups=0,
)


def cost(microseconds):
    size = max(1, int(3e6 * OPT["c"] * microseconds))
    return pl.CostEstimate(flops=1, bytes_accessed=size, transcendentals=0)


def project(place, normed, shards):
    length, width = normed.shape[0], shards[0].shape[1]
    return pl.pallas_call(
        project_kernel,
        out_shape=jax.ShapeDtypeStruct((length, width), BF16),
        in_specs=[smem()] + [vmem()] * (1 + len(shards)),
        out_specs=vmem(),
        compiler_params=params(),
        cost_estimate=cost(1),
        name="project_queries",
    )(place, normed, *shards)


def load_kernel(info, pages, *refs, slots, page):
    outs, sems = refs[:-1], refs[-1]
    tiles = [(k, slot) for k in range(len(outs)) for slot in range(slots)]

    def fetch(k, slot):
        rows = pl.ds(slot * page, page)
        return pltpu.make_async_copy(
            pages.at[info[k, 0], rows], outs[k].at[rows], sems.at[k, slot]
        )

    for k, slot in tiles:
        pl.when(slot < info[k, 1])(lambda k=k, slot=slot: fetch(k, slot).start())
    for k, slot in tiles:
        pl.when(slot < info[k, 1])(lambda k=k, slot=slot: fetch(k, slot).wait())


def load_pages(info, pages, slots):
    blocks, span, _, width = pages.shape
    kernel = functools.partial(load_kernel, slots=slots, page=span // slots)
    return pl.pallas_call(
        kernel,
        out_shape=(jax.ShapeDtypeStruct((span, 2, width), BF16),) * blocks,
        in_specs=[smem(), pl.BlockSpec(memory_space=pltpu.HBM)],
        out_specs=(vmem(),) * blocks,
        scratch_shapes=[pltpu.SemaphoreType.DMA((blocks, slots))],
        compiler_params=params(LOAD_LIMIT),
        cost_estimate=cost(4),
        name="load_pages",
    )(info, pages)


def pool_kernel(info, query, pages, *refs, which, slots, page, heads, length, width):
    ins = refs[:-4]
    out, cache, own, own_lse = refs[-4:]
    used, remain = info[which, 1], info[which, 2]
    lanes_at = lax.broadcasted_iota(jnp.int32, (length, 128), 1)

    @pl.when(used == 0)
    def _():
        own[...] = jnp.zeros(own.shape, F32)
        own_lse[...] = jnp.full(own_lse.shape, EMPTY, F32)

    for count in range(1, slots + 1):

        @pl.when(used == count)
        def _(count=count):
            span = count * page
            cache[:span] = pages[:span].reshape(span, 2 * width)
            columns = lax.broadcasted_iota(jnp.int32, (length, page), 1)
            table = jnp.zeros((length, 128), F32)
            for head in range(heads):
                lanes = slice(head * HD, (head + 1) * HD)
                after = slice(width + head * HD, width + (head + 1) * HD)
                scores = nt(query[:, lanes], cache[:span, lanes])
                last = jnp.where(columns < remain, scores[:, span - page :], EMPTY)
                if count > 1:
                    scores = jnp.concatenate([scores[:, : span - page], last], axis=1)
                else:
                    scores = last
                top = jnp.max(scores, axis=1, keepdims=True)
                probs = jnp.exp2((scores - top) * SCALE)
                total = jnp.sum(probs, axis=1, keepdims=True)
                mixed = nn(probs.astype(BF16), cache[:span, after])
                own[:, lanes] = mixed / total
                table = jnp.where(lanes_at == head, top * SCALE + jnp.log2(total), table)
            own_lse[...] = table

    lse = to_rows(own_lse[...], heads)
    if not ins:
        out[:length, :] = own[...].astype(BF16)
        write_stats(out, length, width, lse)
        return
    stats = [lse] + [read_stats(ref, length, width, heads) for ref in ins]
    weights, merged = merge_weights(stats)
    for head in range(heads):
        lanes = slice(head * HD, (head + 1) * HD)
        mixed = weights[head][0] * own[:, lanes]
        for weight, ref in zip(weights[head][1:], ins):
            mixed = mixed + weight * ref[:length, lanes].astype(F32)
        out[:length, lanes] = mixed.astype(BF16)
    write_stats(out, length, width, merged)


def pool_attend(which, info, query, pages, parts, slots, page):
    length, width = query.shape
    span = slots * page
    kernel = functools.partial(
        pool_kernel,
        which=which,
        slots=slots,
        page=page,
        heads=width // HD,
        length=length,
        width=width,
    )
    return pl.pallas_call(
        kernel,
        out_shape=jax.ShapeDtypeStruct((length + STAT, width), BF16),
        in_specs=[smem()] + [vmem()] * (2 + len(parts)),
        out_specs=vmem(),
        scratch_shapes=[
            pltpu.VMEM((span, 2 * width), BF16),
            pltpu.VMEM((length, width), F32),
            pltpu.VMEM((length, 128), F32),
        ],
        compiler_params=params(),
        cost_estimate=cost(3),
        name="pool_attention",
    )(info, query, pages, *parts)


def merge_kernel(*refs, length, width, heads):
    ins, out = refs[:-1], refs[-1]
    weights, merged = merge_weights([read_stats(ref, length, width, heads) for ref in ins])
    for head in range(heads):
        lanes = slice(head * HD, (head + 1) * HD)
        terms = [w * ref[:length, lanes].astype(F32) for w, ref in zip(weights[head], ins)]
        out[:length, lanes] = functools.reduce(jnp.add, terms).astype(BF16)
    write_stats(out, length, width, merged)


def merge_parts(parts, length, width):
    kernel = functools.partial(merge_kernel, length=length, width=width, heads=width // HD)
    return pl.pallas_call(
        kernel,
        out_shape=jax.ShapeDtypeStruct((length + STAT, width), BF16),
        in_specs=[vmem()] * len(parts),
        out_specs=vmem(),
        compiler_params=params(),
        cost_estimate=cost(2),
        name="merge_partials",
    )(*parts)


def hp(a, b, dims):
    def halves(x):
        high = x.astype(BF16)
        return high, (x - high.astype(F32)).astype(BF16)

    def dot(x, y):
        return lax.dot_general(x, y, (dims, ((), ())), preferred_element_type=F32)

    a_high, a_low = halves(a)
    b_high, b_low = halves(b)
    return dot(a_high, b_high) + (dot(a_high, b_low) + dot(a_low, b_high))


def feature_parts(place, normed, count, depth):
    owners = [lax.rem(place[0] - step + count, count) for step in range(count)]
    return [normed[:, pl.ds(pl.multiple_of(o * depth, depth), depth)] for o in owners]


def weight_tile(place, pieces, step, matrix):
    here = pieces[step - 1]
    share = 4 // len(here)
    turn = lax.rem(place[2] - matrix // share + len(here), len(here))
    chosen = here[0][matrix % share]
    for t in range(1, len(here)):
        chosen = jnp.where(turn == t, here[t][matrix % share], chosen)
    return chosen


def regroup(refs, row):
    groups = len(refs) // (row - 1)
    return [refs[i * groups : (i + 1) * groups] for i in range(row - 1)]


def projected(place, parts, w_own, pieces, matrix):
    terms = [nn(parts[0], w_own[1 + matrix])]
    terms += [
        nn(parts[step], weight_tile(place, pieces, step, matrix)) for step in range(1, len(parts))
    ]
    return functools.reduce(jnp.add, terms)


def local_kernel(
    place,
    scales,
    normed,
    query,
    persist_in,
    memory_in,
    w_own,
    *refs,
    row,
    length,
    heads,
):
    pieces = regroup(refs[:-9], row)
    attended, lse_out, recalled, memory_out, keys, values, memory, persist, sems = refs[-9:]
    loads = [
        pltpu.make_async_copy(persist_in, persist, sems.at[0]),
        pltpu.make_async_copy(memory_in.at[0], memory, sems.at[1]),
    ]
    for load in loads:
        load.start()
    parts = feature_parts(place, normed, row, w_own.shape[1])
    keys[...] = projected(place, parts, w_own, pieces, 0).astype(BF16)
    values[...] = projected(place, parts, w_own, pieces, 1).astype(BF16)
    loads[0].wait()
    rows = 256
    columns_lse = []
    for head in range(heads):
        lanes = slice(head * HD, (head + 1) * HD)
        pieces = []
        for part in range(length // rows):
            rs = slice(part * rows, (part + 1) * rows)
            span = (part + 1) * rows
            scores = nt(query[rs, lanes], keys[:span, lanes])
            own = part * rows + lax.broadcasted_iota(jnp.int32, (rows, span), 0)
            theirs = lax.broadcasted_iota(jnp.int32, (rows, span), 1)
            scores = jnp.where(own >= theirs, scores, EMPTY)
            fixed = nt(query[rs, lanes], persist[0, :, lanes])
            top = jnp.maximum(
                jnp.max(scores, axis=1, keepdims=True), jnp.max(fixed, axis=1, keepdims=True)
            )
            probs = jnp.exp2((scores - top) * SCALE)
            fixed_probs = jnp.exp2((fixed - top) * SCALE)
            total = jnp.sum(probs, axis=1, keepdims=True) + jnp.sum(
                fixed_probs, axis=1, keepdims=True
            )
            mixed = nn(probs.astype(BF16), values[:span, lanes]) + nn(
                fixed_probs.astype(BF16), persist[1, :, lanes]
            )
            attended[rs, lanes] = mixed / total
            pieces.append(top * SCALE + jnp.log2(total))
        columns_lse.append(jnp.concatenate(pieces, axis=0))
    lanes_at = lax.broadcasted_iota(jnp.int32, (length, 128), 1)
    table = jnp.zeros((length, 128), F32)
    for head in range(heads):
        table = jnp.where(lanes_at == head, columns_lse[head], table)
    lse_out[...] = stack_rows(to_rows(table, heads))

    loads[1].wait()

    def update(segment, carry):
        rs = pl.ds(pl.multiple_of(segment * SEG, SEG), SEG)
        for head in range(heads):
            lanes = slice(head * HD, (head + 1) * HD)
            seg_query = query[rs, lanes].astype(F32)
            seg_keys = keys[rs, lanes].astype(F32)
            seg_query = seg_query * lax.rsqrt(
                jnp.sum(seg_query * seg_query, axis=1, keepdims=True) + 1e-06
            )
            seg_keys = seg_keys * lax.rsqrt(
                jnp.sum(seg_keys * seg_keys, axis=1, keepdims=True) + 1e-06
            )
            state = memory[head]
            both = hp(jnp.concatenate([seg_query, seg_keys], axis=0), state, ((1,), (0,)))
            recalled[rs, lanes] = both[:SEG]
            errors = both[SEG:] - values[rs, lanes].astype(F32)
            change = hp(seg_keys, errors, ((0,), (0,)))
            memory[head] = scales[0, segment, head] * state - scales[1, segment, head] * change
        return carry

    lax.fori_loop(0, length // SEG, update, 0, unroll=True)
    memory_out[0] = memory[...]


def local_part(place, scales, normed, query, persist, memory, w_own, pieces, row):
    length, width = query.shape
    heads = width // HD
    kernel = functools.partial(local_kernel, row=row, length=length, heads=heads)
    return pl.pallas_call(
        kernel,
        out_shape=(
            jax.ShapeDtypeStruct((length, width), F32),
            jax.ShapeDtypeStruct((8, length), F32),
            jax.ShapeDtypeStruct((length, width), F32),
            jax.ShapeDtypeStruct(memory.shape, F32),
        ),
        in_specs=[smem()] * 2
        + [vmem()] * 2
        + [pl.BlockSpec(memory_space=pltpu.HBM)] * 2
        + [vmem()] * (1 + len(pieces)),
        out_specs=(vmem(),) * 4,
        scratch_shapes=[
            pltpu.VMEM((length, width), BF16),
            pltpu.VMEM((length, width), BF16),
            pltpu.VMEM((heads, HD, HD), F32),
            pltpu.VMEM(persist.shape, BF16),
            pltpu.SemaphoreType.DMA((2,)),
        ],
        compiler_params=params(),
        cost_estimate=cost(6),
        name="local_part",
    )(place, scales, normed, query, persist, memory, w_own, *pieces)


def early_kernel(
    place, normed, w_own, recalled, attended, lse_in, *refs, count, row, length, width
):
    pieces, ins = regroup(refs[:count], row), refs[count:-3]
    mixed_out, lse_out, gated = refs[-3:]
    heads = width // HD
    parts = feature_parts(place, normed, row, w_own.shape[1])
    gated[...] = jax.nn.sigmoid(projected(place, parts, w_own, pieces, 2)) * recalled[...]
    own = [lse_in[head : head + 1, :] for head in range(heads)]
    weights, merged = merge_weights(
        [own] + [read_stats(ref, length, width, heads) for ref in ins]
    )
    for head in range(heads):
        lanes = slice(head * HD, (head + 1) * HD)
        mixed = weights[head][0] * attended[:, lanes]
        for weight, ref in zip(weights[head][1:], ins):
            mixed = mixed + weight * ref[:length, lanes].astype(F32)
        mixed_out[:, lanes] = mixed
    lse_out[...] = stack_rows(merged)


def early_part(place, normed, w_own, pieces, row, recalled, attended, lse, parts):
    length, width = attended.shape
    kernel = functools.partial(
        early_kernel, count=len(pieces), row=row, length=length, width=width
    )
    full = jax.ShapeDtypeStruct((length, width), F32)
    return pl.pallas_call(
        kernel,
        out_shape=(full, jax.ShapeDtypeStruct(lse.shape, F32), full),
        in_specs=[smem()] + [vmem()] * (5 + len(pieces) + len(parts)),
        out_specs=(vmem(),) * 3,
        compiler_params=params(),
        cost_estimate=cost(4),
        name="early_part",
    )(place, normed, w_own, recalled, attended, lse, *pieces, *parts)


def final_kernel(place, attended, lse_in, gated, w_own, *refs, sources, row, length, width):
    pieces, ins = regroup(refs[:sources], row), refs[sources:-3]
    send, keep, combined = refs[-3:]
    heads = width // HD
    count = row
    own = [lse_in[head : head + 1, :] for head in range(heads)]
    weights, _ = merge_weights([own] + [read_stats(ref, length, width, heads) for ref in ins])
    for head in range(heads):
        lanes = slice(head * HD, (head + 1) * HD)
        mixed = weights[head][0] * attended[:, lanes]
        for weight, ref in zip(weights[head][1:], ins):
            mixed = mixed + weight * ref[:length, lanes].astype(F32)
        combined[:, lanes] = (mixed + gated[:, lanes]).astype(BF16)
    for step in range(count):
        owner = lax.rem(place[0] - step + count, count)
        tile = w_own[4] if step == 0 else weight_tile(place, pieces, step, 3)
        term = nt(combined[...], tile).astype(BF16)
        other = lax.rem(owner + place[1], 2)
        where = lax.div(owner, 2)

        @pl.when(other == 1)
        def _():
            send[where] = term

        @pl.when(other == 0)
        def _():
            keep[where] = term


def final_part(place, attended, lse, gated, parts, w_own, pieces, row):
    length, width = attended.shape
    kernel = functools.partial(
        final_kernel, sources=len(pieces), row=row, length=length, width=width
    )
    count = row
    half = jax.ShapeDtypeStruct((count // 2, length, w_own.shape[1]), BF16)
    return pl.pallas_call(
        kernel,
        out_shape=(half, half),
        in_specs=[smem()] + [vmem()] * (4 + len(pieces) + len(parts)),
        out_specs=(vmem(), vmem()),
        scratch_shapes=[pltpu.VMEM((length, width), BF16)],
        compiler_params=params(),
        cost_estimate=cost(3),
        name="final_part",
    )(place, attended, lse, gated, w_own, *pieces, *parts)


def pair_kernel(place, tokens, keep, got, mine, away):
    spot = lax.div(place[1], 2)
    mine[...] = tokens[...].astype(F32) + (keep[spot].astype(F32) + got[spot].astype(F32))
    for step in range(1, keep.shape[0]):
        other = jnp.bitwise_xor(spot, step)
        away[step - 1] = (keep[other].astype(F32) + got[other].astype(F32)).astype(BF16)


def pair_sum(place, tokens, keep, got):
    count, length, width = keep.shape
    return pl.pallas_call(
        pair_kernel,
        out_shape=(
            jax.ShapeDtypeStruct((length, width), F32),
            jax.ShapeDtypeStruct((count - 1, length, width), BF16),
        ),
        in_specs=[smem()] + [vmem()] * 3,
        out_specs=(vmem(), vmem()),
        compiler_params=params(),
        cost_estimate=cost(1),
        name="pair_sum",
    )(place, tokens, keep, got)


def shards(tokens, norm_gain, w_attn, persist_kv, kv_pool, cache_len, mem_state, decay, rate):
    req, row, col = lax.axis_size("req"), lax.axis_size("row"), lax.axis_size("col")
    pool_size = req * row
    my_req, my_row, my_col = lax.axis_index("req"), lax.axis_index("row"), lax.axis_index("col")
    my_index = my_req * row + my_row
    length = tokens.shape[0]
    width = w_attn.shape[2]
    slots, page = kv_pool.shape[2], kv_pool.shape[3]

    def shift(x, axis, by, name):
        size = lax.axis_size(axis)
        with jax.named_scope(name):
            return lax.ppermute(x, axis, [(i, (i + by) % size) for i in range(size)])

    def after(x, *others):
        return lax.optimization_barrier((x,) + others)[0]

    w_query = w_attn[0]
    query_shards = [w_query] + [
        shift(w_query, "row", s, f"query_weights_{s}") for s in range(1, row)
    ]
    xfloat = tokens.astype(F32)
    normed = (
        xfloat * lax.rsqrt(jnp.mean(xfloat * xfloat, axis=-1, keepdims=True) + 1e-05) * norm_gain
    ).astype(BF16)
    scales = jnp.stack([decay[0], rate[0]])
    own_width = tokens.shape[1] // col
    own_cols = lax.dynamic_slice_in_dim(tokens, my_col * own_width, own_width, 1)
    groups = min(req, 4) if OPT["groups"] else 1
    group = my_req % groups
    place = jnp.stack([my_row, my_col, group]).astype(jnp.int32)

    order = [0] + list(dict.fromkeys([s for s in (1, row - 1) if 0 < s < row] + list(range(1, row))))
    steps = jnp.asarray(order, jnp.int32)[:, None]
    turns = jnp.arange(req, dtype=jnp.int32)[None, :]
    blocks = (((my_req - turns) % req) * row + (my_row - steps) % row).reshape(-1)
    offsets = (my_index - blocks) % pool_size
    limits = cache_len[blocks]
    used = jnp.clip(
        ((limits + page - 1) // page - offsets + pool_size - 1) // pool_size, 0, slots
    )
    last = (used - 1) * pool_size + offsets
    info = jnp.stack([blocks, used, limits - last * page], axis=1).astype(jnp.int32)

    pages = kv_pool[0].reshape(pool_size, slots * page, 2, width)
    place, scales, own_cols = lax.optimization_barrier((place, scales, own_cols))
    if OPT["lay"] == 1:
        pages = load_pages(info, pages, slots)
        place = after(place, *pages)
    queries = project(place, normed, query_shards)
    if OPT["lay"] == 2:
        pages = load_pages(after(info, queries), pages, slots)

    order = order[1:]
    far = order[-1]
    numbered = {}
    for s in [0] + order:
        for t in range(req):
            numbered[s, t] = len(numbered)
    partials, back, arrived = {}, {}, {}
    latest = [queries]
    outs = []

    def attend(s, t, here, parts=()):
        number = numbered[s, t]
        info_now = after(info, latest[0]) if OPT["kchain"] else info
        latest[0] = partials[s, t] = pool_attend(
            number, info_now, here, pages[number], parts, slots, page
        )
        outs.append(latest[0])

    def send_back(s, *first):
        back[s] = [
            shift(after(partials[s, t], *first), "req", -t, f"partials_req_{s}")
            for t in range(1, req)
        ]

    def merge_arrived(s, *first):
        if (s, 0) not in partials:
            attend(s, 0, after(by_row[s], *first), back[s])
            arrived[s] = latest[0]
            return
        if OPT["kchain"]:
            first = (latest[0],) + first
        parts = [after(partials[s, 0], *first)] + back[s]
        latest[0] = arrived[s] = merge_parts(parts, length, width)

    def over_row(x, name, relay, *first):
        got = {}
        for s in order:
            if s in (1, row - 1) or not relay:
                got[s] = shift(x, "row", s, f"{name}_row_{s}")
            else:
                moved = after(got[s - 1], *first)
                got[s] = shift(moved, "row", 1, f"{name}_row_{s}")
        return got

    def over_req(x, name, *first):
        return [shift(after(x, *first), "req", t, name) for t in range(1, req)]

    by_row = over_row(queries, "queries", OPT["relayq"])
    by_row[0] = queries
    there = {0: over_req(queries, "queries_req_0")}
    sequence = [(0, 0)] + [(0, t) for t in range(1, req)]
    if OPT["korder"] == 0:
        for s in order:
            sequence += [(s, t) for t in range(req)]
    elif OPT["korder"] == 1:
        sequence += [(s, 0) for s in order[:-1]]
        sequence += [(s, t) for s in order[:-1] for t in range(1, req)]
        sequence += [(order[-1], t) for t in range(req)]
    elif OPT["korder"] >= 4:
        one, near = order[0], order[1:-1]
        sequence = [(0, 0), (one, 0)] + [(0, t) for t in range(1, req)]
        sequence += [(one, t) for t in range(1, req)]
        if OPT["korder"] == 6:
            sequence += [(s, t) for s in near + [far] for t in range(1, req)]
            sequence += [(s, 0) for s in near + [far]]
        elif OPT["korder"] == 7:
            sequence += [(s, t) for s in [far] + near for t in range(1, req)]
            sequence += [(s, 0) for s in near + [far]]
        elif OPT["korder"] == 4:
            sequence += [(far, 0)] + [(s, t) for s in near for t in range(req)]
            sequence += [(far, t) for t in range(1, req)]
        else:
            sequence += [(s, 0) for s in near] + [(far, 0)]
            sequence += [(far, t) for t in range(1, req)]
            sequence += [(s, t) for s in near for t in range(1, req)]
    elif OPT["korder"] == 2:
        sequence = [(0, 0)] + [(s, 0) for s in order[:1]] + [(0, t) for t in range(1, req)]
        sequence += [(s, t) for s in order[:1] for t in range(1, req)]
        for s in order[1:]:
            sequence += [(s, t) for t in range(req)]
    else:
        sequence = [(0, 0)] + [(s, 0) for s in order[:1]]
        sequence += [(s, t) for s in order[:1] for t in range(1, req)]
        for s in order[1:]:
            sequence += [(s, t) for t in range(req)]
        sequence += [(0, t) for t in range(1, req)]
    fused = order[len(order) - OPT["fuse"] :]
    sequence = [(s, t) for s, t in sequence if t or s not in fused]
    when = {0: -1}
    for i, s in enumerate(order):
        when[s] = i
    for i, (s, t) in enumerate(sequence):
        if i == 1:
            first = outs if OPT["rtie"] == 1 else pages if OPT["rtie"] == 2 else []
            for f in range(2, row - 1):
                moved = after(by_row[f - 1], *first)
                by_row[f] = shift(moved, "row", 1, f"queries_row_{f}")
        if t and s not in there:
            first = []
            if OPT["ytie"] and when[s] >= 0:
                first = [outs[min(when[s], i - 1)]]
                if OPT["ytie"] == 2:
                    first = [outs[{order[0]: 0, far: 3}.get(s, 1)]]
                if OPT["ytie"] == 4:
                    first = [outs[0]]
                if OPT["ytie"] == 5:
                    first = [outs[{far: 0}.get(s, 1)]]
                if OPT["ytie"] == 6:
                    first = [outs[1]]
                if OPT["ytie"] == 3:
                    first = [outs[{order[0]: 0, far: 2}.get(s, 1)]]
            there[s] = over_req(by_row[s], f"queries_req_{s}", *first)
            if OPT["ytie"] > 1 and s == order[0]:
                for other in order[1:]:
                    if OPT["ytie"] < 4 and other == far:
                        continue
                    late = OPT["ytie"] < 4 or (OPT["ytie"] == 5 and other != far)
                    first = [outs[1 if late or OPT["ytie"] == 6 else 0]]
                    there[other] = over_req(by_row[other], f"queries_req_{other}", *first)
        attend(s, t, there[s][t - 1] if t else by_row[s])
    for s in order:
        first = []
        if OPT["ptie"] and s == far:
            first = [part for done in order[:-1] for part in back[done]]
        send_back(s, *first)

    share = 4 // groups
    w_share = lax.dynamic_slice_in_dim(w_attn, 1 + group * share, share, 0)
    ties = dict(
        q=[queries],
        near=[by_row[order[0]]],
        near2=[by_row[s] for s in order[:2]],
        far=[by_row[far]],
        all=[by_row[s] for s in order] + [outs[2]],
        k4=[outs[min(4, len(outs) - 1)]],
    )
    fetched = over_row(after(w_share, *ties[OPT["wtie"]]), "weights", OPT["relayw"])
    pieces = []
    for s in range(1, row):
        moved = fetched[s]
        if OPT["wytie"] == 1:
            moved = after(moved, outs[-1])
        elif OPT["wytie"] == 2:
            moved = after(moved, *back[far])
        elif OPT["wytie"] == 3 and s not in (1, row - 1):
            moved = after(moved, *back[far])
        pieces += [fetched[s]] + [
            shift(moved, "req", t, f"weights_req_{s}") for t in range(1, groups)
        ]
    for s in order if OPT["morder"] == 0 else order[::-1]:
        first = []
        if OPT["mtie"] == 1 and s == order[0]:
            first = [fetched[far]]
        if OPT["mtie"] == 2 and s == far:
            first = [fetched[far]]
        if OPT["wk"] and s == far:
            first = first + [pieces[groups * k + 1] for k in (0, row - 2)[: OPT["wk"]] if groups > 1]
        if OPT["ztie"] and s == far and s != order[0]:
            first = first + [arrived[order[0]]]
        merge_arrived(s, *first)
        merged_last = latest[0]
        arrived[s] = shift(arrived[s], "row", -s, f"partials_row_{s}")
    send_back(0, *([merged_last] if OPT["p0"] == 1 else [] if OPT["p0"] == 0 else [outs[-1]]))
    if not OPT["loc"]:
        merged_last = queries

    local_out, local_lse, recalled, new_state = local_part(
        place,
        scales,
        normed,
        after(queries, merged_last),
        persist_kv,
        mem_state,
        w_attn,
        pieces,
        row,
    )
    early = [partials[0, 0]] + back[0] + [arrived[s] for s in order[:-1]]
    mixed, lse, gated = early_part(
        place, normed, w_attn, pieces, row, recalled, local_out, local_lse, early
    )
    send, keep = final_part(place, mixed, lse, gated, [arrived[far]], w_attn, pieces, row)
    with jax.named_scope("output_pairs"):
        got = lax.ppermute(send, "col", [(i, i ^ 1) for i in range(col)])
    mine, away = pair_sum(place, own_cols, keep, got)
    for step in range(1, col // 2):
        with jax.named_scope("output_quarters"):
            came = lax.ppermute(away[step - 1], "col", [(i, i ^ (2 * step)) for i in range(col)])
        mine = mine + came.astype(F32)
    return (mine.astype(BF16), new_state)


def solution(mesh):
    return jax.shard_map(
        shards,
        mesh=mesh,
        in_specs=(
            P(("req", "row"), None),
            P(),
            P(None, "row", "col"),
            P(None, None, "col"),
            P(("req", "row"), None, None, None, None, "col"),
            P(),
            P(("req", "row"), "col", None, None),
            P(("req", "row"), None, "col"),
            P(("req", "row"), None, "col"),
        ),
        out_specs=(P(("req", "row"), "col"), P(("req", "row"), "col", None, None)),
        check_vma=False,
    )
```

```python
import functools

import jax
import jax.numpy as jnp
from jax import lax
from jax.experimental import pallas as pl
from jax.experimental.pallas import tpu as pltpu
from jax.sharding import PartitionSpec as P

HD = 128
NP = 16
SEG = 64
LOG2E = 1.4426950408889634
SCALE = HD ** (-0.5) * LOG2E
EMPTY = -1e30
STAT = 16
F32 = jnp.float32
BF16 = jnp.bfloat16
VMEM_LIMIT = 16 * 1024 * 1024
LOAD_LIMIT = 52 * 1024 * 1024


def nt(a, b):
    return lax.dot_general(a, b, (((1,), (1,)), ((), ())), preferred_element_type=F32)


def nn(a, b):
    return lax.dot_general(a, b, (((1,), (0,)), ((), ())), preferred_element_type=F32)


def split3(x):
    high = x.astype(BF16).astype(F32)
    rest = x - high
    middle = rest.astype(BF16).astype(F32)
    return high, middle, (rest - middle).astype(BF16).astype(F32)


def stack_rows(rows, count=8):
    length = rows[0].shape[1]
    spots = lax.broadcasted_iota(jnp.int32, (count, length), 0)
    table = jnp.zeros((count, length), F32)
    for spot, row in enumerate(rows):
        table = jnp.where(spots == spot, row, table)
    return table


def to_columns(rows):
    length = rows[0].shape[1]
    count = (len(rows) + 7) // 8 * 8
    table = jnp.concatenate(
        [stack_rows(rows, count), jnp.zeros((128 - count, length), F32)], axis=0
    )
    table = jnp.transpose(table)
    return [table[:, spot : spot + 1] for spot in range(len(rows))]


def to_rows(table, heads):
    rows = jnp.transpose(table)[:8]
    return [rows[head : head + 1] for head in range(heads)]


def write_stats(out_ref, length, width, lse):
    rows = stack_rows([piece for row in lse for piece in split3(row)])
    parts = length // width
    packed = jnp.concatenate(
        [rows[:, part * width : (part + 1) * width] for part in range(parts)], axis=0
    )
    out_ref[length : length + 8 * parts, :] = packed.astype(BF16)


def read_stats(ref, length, width, heads):
    parts = length // width
    packed = ref[length : length + 8 * parts, :].astype(F32)
    rows = jnp.concatenate([packed[8 * part : 8 * part + 8] for part in range(parts)], axis=1)
    return [
        rows[3 * head : 3 * head + 1]
        + rows[3 * head + 1 : 3 * head + 2]
        + rows[3 * head + 2 : 3 * head + 3]
        for head in range(heads)
    ]


def merge_weights(stats):
    rows, merged = [], []
    heads = len(stats[0])
    for head in range(heads):
        lse = [stat[head] for stat in stats]
        top = functools.reduce(jnp.maximum, lse)
        weights = [jnp.exp2(one - top) for one in lse]
        total = functools.reduce(jnp.add, weights)
        rows += [weight / total for weight in weights]
        merged.append(top + jnp.log2(total))
    columns = to_columns(rows)
    count = len(stats)
    return [columns[head * count : (head + 1) * count] for head in range(heads)], merged


def project_kernel(place, normed, *refs):
    shards, out = refs[:-1], refs[-1]
    depth = shards[0].shape[0]
    count = len(shards)
    total = None
    for step in range(count):
        owner = lax.rem(place[0] - step + count, count)
        part = normed[:, pl.ds(pl.multiple_of(owner * depth, depth), depth)]
        term = nn(part, shards[step][...])
        total = term if total is None else total + term
    out[...] = total.astype(BF16)


def smem():
    return pl.BlockSpec(memory_space=pltpu.SMEM)


def vmem():
    return pl.BlockSpec(memory_space=pltpu.VMEM)


def params(limit=VMEM_LIMIT):
    return pltpu.CompilerParams(vmem_limit_bytes=limit)


OPT = dict(
    c=0.3, kchain=1, korder=4, ytie=2, wtie="near2", wytie=0, mtie=0, loc=0, relayq=1, relayw=1,
    p0=2, ztie=0, wk=0, lay=2, ptie=0, rtie=2, fuse=2, morder=0, groups=0,
)


def cost(microseconds):
    size = max(1, int(3e6 * OPT["c"] * microseconds))
    return pl.CostEstimate(flops=1, bytes_accessed=size, transcendentals=0)


def project(place, normed, shards):
    length, width = normed.shape[0], shards[0].shape[1]
    return pl.pallas_call(
        project_kernel,
        out_shape=jax.ShapeDtypeStruct((length, width), BF16),
        in_specs=[smem()] + [vmem()] * (1 + len(shards)),
        out_specs=vmem(),
        compiler_params=params(),
        cost_estimate=cost(1),
        name="project_queries",
    )(place, normed, *shards)


def load_kernel(info, pages, *refs, slots, page):
    outs, sems = refs[:-1], refs[-1]
    tiles = [(k, slot) for k in range(len(outs)) for slot in range(slots)]

    def fetch(k, slot):
        rows = pl.ds(slot * page, page)
        return pltpu.make_async_copy(
            pages.at[info[k, 0], rows], outs[k].at[rows], sems.at[k, slot]
        )

    for k, slot in tiles:
        pl.when(slot < info[k, 1])(lambda k=k, slot=slot: fetch(k, slot).start())
    for k, slot in tiles:
        pl.when(slot < info[k, 1])(lambda k=k, slot=slot: fetch(k, slot).wait())


def load_pages(info, pages, slots):
    blocks, span, _, width = pages.shape
    kernel = functools.partial(load_kernel, slots=slots, page=span // slots)
    return pl.pallas_call(
        kernel,
        out_shape=(jax.ShapeDtypeStruct((span, 2, width), BF16),) * blocks,
        in_specs=[smem(), pl.BlockSpec(memory_space=pltpu.HBM)],
        out_specs=(vmem(),) * blocks,
        scratch_shapes=[pltpu.SemaphoreType.DMA((blocks, slots))],
        compiler_params=params(LOAD_LIMIT),
        cost_estimate=cost(4),
        name="load_pages",
    )(info, pages)


def pool_kernel(info, query, pages, *refs, which, slots, page, heads, length, width):
    ins = refs[:-4]
    out, cache, own, own_lse = refs[-4:]
    used, remain = info[which, 1], info[which, 2]
    lanes_at = lax.broadcasted_iota(jnp.int32, (length, 128), 1)

    @pl.when(used == 0)
    def _():
        own[...] = jnp.zeros(own.shape, F32)
        own_lse[...] = jnp.full(own_lse.shape, EMPTY, F32)

    for count in range(1, slots + 1):

        @pl.when(used == count)
        def _(count=count):
            span = count * page
            cache[:span] = pages[:span].reshape(span, 2 * width)
            columns = lax.broadcasted_iota(jnp.int32, (length, page), 1)
            table = jnp.zeros((length, 128), F32)
            for head in range(heads):
                lanes = slice(head * HD, (head + 1) * HD)
                after = slice(width + head * HD, width + (head + 1) * HD)
                scores = nt(query[:, lanes], cache[:span, lanes])
                last = jnp.where(columns < remain, scores[:, span - page :], EMPTY)
                if count > 1:
                    scores = jnp.concatenate([scores[:, : span - page], last], axis=1)
                else:
                    scores = last
                top = jnp.max(scores, axis=1, keepdims=True)
                probs = jnp.exp2((scores - top) * SCALE)
                total = jnp.sum(probs, axis=1, keepdims=True)
                mixed = nn(probs.astype(BF16), cache[:span, after])
                own[:, lanes] = mixed / total
                table = jnp.where(lanes_at == head, top * SCALE + jnp.log2(total), table)
            own_lse[...] = table

    lse = to_rows(own_lse[...], heads)
    if not ins:
        out[:length, :] = own[...].astype(BF16)
        write_stats(out, length, width, lse)
        return
    stats = [lse] + [read_stats(ref, length, width, heads) for ref in ins]
    weights, merged = merge_weights(stats)
    for head in range(heads):
        lanes = slice(head * HD, (head + 1) * HD)
        mixed = weights[head][0] * own[:, lanes]
        for weight, ref in zip(weights[head][1:], ins):
            mixed = mixed + weight * ref[:length, lanes].astype(F32)
        out[:length, lanes] = mixed.astype(BF16)
    write_stats(out, length, width, merged)


def pool_attend(which, info, query, pages, parts, slots, page):
    length, width = query.shape
    span = slots * page
    kernel = functools.partial(
        pool_kernel,
        which=which,
        slots=slots,
        page=page,
        heads=width // HD,
        length=length,
        width=width,
    )
    return pl.pallas_call(
        kernel,
        out_shape=jax.ShapeDtypeStruct((length + STAT, width), BF16),
        in_specs=[smem()] + [vmem()] * (2 + len(parts)),
        out_specs=vmem(),
        scratch_shapes=[
            pltpu.VMEM((span, 2 * width), BF16),
            pltpu.VMEM((length, width), F32),
            pltpu.VMEM((length, 128), F32),
        ],
        compiler_params=params(),
        cost_estimate=cost(3),
        name="pool_attention",
    )(info, query, pages, *parts)


def merge_kernel(*refs, length, width, heads):
    ins, out = refs[:-1], refs[-1]
    weights, merged = merge_weights([read_stats(ref, length, width, heads) for ref in ins])
    for head in range(heads):
        lanes = slice(head * HD, (head + 1) * HD)
        terms = [w * ref[:length, lanes].astype(F32) for w, ref in zip(weights[head], ins)]
        out[:length, lanes] = functools.reduce(jnp.add, terms).astype(BF16)
    write_stats(out, length, width, merged)


def merge_parts(parts, length, width):
    kernel = functools.partial(merge_kernel, length=length, width=width, heads=width // HD)
    return pl.pallas_call(
        kernel,
        out_shape=jax.ShapeDtypeStruct((length + STAT, width), BF16),
        in_specs=[vmem()] * len(parts),
        out_specs=vmem(),
        compiler_params=params(),
        cost_estimate=cost(2),
        name="merge_partials",
    )(*parts)


def hp(a, b, dims):
    def halves(x):
        high = x.astype(BF16)
        return high, (x - high.astype(F32)).astype(BF16)

    def dot(x, y):
        return lax.dot_general(x, y, (dims, ((), ())), preferred_element_type=F32)

    a_high, a_low = halves(a)
    b_high, b_low = halves(b)
    return dot(a_high, b_high) + (dot(a_high, b_low) + dot(a_low, b_high))


def feature_parts(place, normed, count, depth):
    owners = [lax.rem(place[0] - step + count, count) for step in range(count)]
    return [normed[:, pl.ds(pl.multiple_of(o * depth, depth), depth)] for o in owners]


def weight_tile(place, pieces, step, matrix):
    here = pieces[step - 1]
    share = 4 // len(here)
    turn = lax.rem(place[2] - matrix // share + len(here), len(here))
    chosen = here[0][matrix % share]
    for t in range(1, len(here)):
        chosen = jnp.where(turn == t, here[t][matrix % share], chosen)
    return chosen


def regroup(refs, row):
    groups = len(refs) // (row - 1)
    return [refs[i * groups : (i + 1) * groups] for i in range(row - 1)]


def projected(place, parts, w_own, pieces, matrix):
    terms = [nn(parts[0], w_own[1 + matrix])]
    terms += [
        nn(parts[step], weight_tile(place, pieces, step, matrix)) for step in range(1, len(parts))
    ]
    return functools.reduce(jnp.add, terms)


def local_kernel(
    place,
    scales,
    normed,
    query,
    persist_in,
    memory_in,
    w_own,
    *refs,
    row,
    length,
    heads,
):
    pieces = regroup(refs[:-9], row)
    attended, lse_out, recalled, memory_out, keys, values, memory, persist, sems = refs[-9:]
    loads = [
        pltpu.make_async_copy(persist_in, persist, sems.at[0]),
        pltpu.make_async_copy(memory_in.at[0], memory, sems.at[1]),
    ]
    for load in loads:
        load.start()
    parts = feature_parts(place, normed, row, w_own.shape[1])
    keys[...] = projected(place, parts, w_own, pieces, 0).astype(BF16)
    values[...] = projected(place, parts, w_own, pieces, 1).astype(BF16)
    loads[0].wait()
    rows = 256
    columns_lse = []
    for head in range(heads):
        lanes = slice(head * HD, (head + 1) * HD)
        pieces = []
        for part in range(length // rows):
            rs = slice(part * rows, (part + 1) * rows)
            span = (part + 1) * rows
            scores = nt(query[rs, lanes], keys[:span, lanes])
            own = part * rows + lax.broadcasted_iota(jnp.int32, (rows, span), 0)
            theirs = lax.broadcasted_iota(jnp.int32, (rows, span), 1)
            scores = jnp.where(own >= theirs, scores, EMPTY)
            fixed = nt(query[rs, lanes], persist[0, :, lanes])
            top = jnp.maximum(
                jnp.max(scores, axis=1, keepdims=True), jnp.max(fixed, axis=1, keepdims=True)
            )
            probs = jnp.exp2((scores - top) * SCALE)
            fixed_probs = jnp.exp2((fixed - top) * SCALE)
            total = jnp.sum(probs, axis=1, keepdims=True) + jnp.sum(
                fixed_probs, axis=1, keepdims=True
            )
            mixed = nn(probs.astype(BF16), values[:span, lanes]) + nn(
                fixed_probs.astype(BF16), persist[1, :, lanes]
            )
            attended[rs, lanes] = mixed / total
            pieces.append(top * SCALE + jnp.log2(total))
        columns_lse.append(jnp.concatenate(pieces, axis=0))
    lanes_at = lax.broadcasted_iota(jnp.int32, (length, 128), 1)
    table = jnp.zeros((length, 128), F32)
    for head in range(heads):
        table = jnp.where(lanes_at == head, columns_lse[head], table)
    lse_out[...] = stack_rows(to_rows(table, heads))

    loads[1].wait()

    def update(segment, carry):
        rs = pl.ds(pl.multiple_of(segment * SEG, SEG), SEG)
        for head in range(heads):
            lanes = slice(head * HD, (head + 1) * HD)
            seg_query = query[rs, lanes].astype(F32)
            seg_keys = keys[rs, lanes].astype(F32)
            seg_query = seg_query * lax.rsqrt(
                jnp.sum(seg_query * seg_query, axis=1, keepdims=True) + 1e-06
            )
            seg_keys = seg_keys * lax.rsqrt(
                jnp.sum(seg_keys * seg_keys, axis=1, keepdims=True) + 1e-06
            )
            state = memory[head]
            both = hp(jnp.concatenate([seg_query, seg_keys], axis=0), state, ((1,), (0,)))
            recalled[rs, lanes] = both[:SEG]
            errors = both[SEG:] - values[rs, lanes].astype(F32)
            change = hp(seg_keys, errors, ((0,), (0,)))
            memory[head] = scales[0, segment, head] * state - scales[1, segment, head] * change
        return carry

    lax.fori_loop(0, length // SEG, update, 0, unroll=True)
    memory_out[0] = memory[...]


def local_part(place, scales, normed, query, persist, memory, w_own, pieces, row):
    length, width = query.shape
    heads = width // HD
    kernel = functools.partial(local_kernel, row=row, length=length, heads=heads)
    return pl.pallas_call(
        kernel,
        out_shape=(
            jax.ShapeDtypeStruct((length, width), F32),
            jax.ShapeDtypeStruct((8, length), F32),
            jax.ShapeDtypeStruct((length, width), F32),
            jax.ShapeDtypeStruct(memory.shape, F32),
        ),
        in_specs=[smem()] * 2
        + [vmem()] * 2
        + [pl.BlockSpec(memory_space=pltpu.HBM)] * 2
        + [vmem()] * (1 + len(pieces)),
        out_specs=(vmem(),) * 4,
        scratch_shapes=[
            pltpu.VMEM((length, width), BF16),
            pltpu.VMEM((length, width), BF16),
            pltpu.VMEM((heads, HD, HD), F32),
            pltpu.VMEM(persist.shape, BF16),
            pltpu.SemaphoreType.DMA((2,)),
        ],
        compiler_params=params(),
        cost_estimate=cost(6),
        name="local_part",
    )(place, scales, normed, query, persist, memory, w_own, *pieces)


def early_kernel(
    place, normed, w_own, recalled, attended, lse_in, *refs, count, row, length, width
):
    pieces, ins = regroup(refs[:count], row), refs[count:-3]
    mixed_out, lse_out, gated = refs[-3:]
    heads = width // HD
    parts = feature_parts(place, normed, row, w_own.shape[1])
    gated[...] = jax.nn.sigmoid(projected(place, parts, w_own, pieces, 2)) * recalled[...]
    own = [lse_in[head : head + 1, :] for head in range(heads)]
    weights, merged = merge_weights(
        [own] + [read_stats(ref, length, width, heads) for ref in ins]
    )
    for head in range(heads):
        lanes = slice(head * HD, (head + 1) * HD)
        mixed = weights[head][0] * attended[:, lanes]
        for weight, ref in zip(weights[head][1:], ins):
            mixed = mixed + weight * ref[:length, lanes].astype(F32)
        mixed_out[:, lanes] = mixed
    lse_out[...] = stack_rows(merged)


def early_part(place, normed, w_own, pieces, row, recalled, attended, lse, parts):
    length, width = attended.shape
    kernel = functools.partial(
        early_kernel, count=len(pieces), row=row, length=length, width=width
    )
    full = jax.ShapeDtypeStruct((length, width), F32)
    return pl.pallas_call(
        kernel,
        out_shape=(full, jax.ShapeDtypeStruct(lse.shape, F32), full),
        in_specs=[smem()] + [vmem()] * (5 + len(pieces) + len(parts)),
        out_specs=(vmem(),) * 3,
        compiler_params=params(),
        cost_estimate=cost(4),
        name="early_part",
    )(place, normed, w_own, recalled, attended, lse, *pieces, *parts)


def final_kernel(place, attended, lse_in, gated, w_own, *refs, sources, row, length, width):
    pieces, ins = regroup(refs[:sources], row), refs[sources:-3]
    send, keep, combined = refs[-3:]
    heads = width // HD
    count = row
    own = [lse_in[head : head + 1, :] for head in range(heads)]
    weights, _ = merge_weights([own] + [read_stats(ref, length, width, heads) for ref in ins])
    for head in range(heads):
        lanes = slice(head * HD, (head + 1) * HD)
        mixed = weights[head][0] * attended[:, lanes]
        for weight, ref in zip(weights[head][1:], ins):
            mixed = mixed + weight * ref[:length, lanes].astype(F32)
        combined[:, lanes] = (mixed + gated[:, lanes]).astype(BF16)
    for step in range(count):
        owner = lax.rem(place[0] - step + count, count)
        tile = w_own[4] if step == 0 else weight_tile(place, pieces, step, 3)
        term = nt(combined[...], tile).astype(BF16)
        other = lax.rem(owner + place[1], 2)
        where = lax.div(owner, 2)

        @pl.when(other == 1)
        def _():
            send[where] = term

        @pl.when(other == 0)
        def _():
            keep[where] = term


def final_part(place, attended, lse, gated, parts, w_own, pieces, row):
    length, width = attended.shape
    kernel = functools.partial(
        final_kernel, sources=len(pieces), row=row, length=length, width=width
    )
    count = row
    half = jax.ShapeDtypeStruct((count // 2, length, w_own.shape[1]), BF16)
    return pl.pallas_call(
        kernel,
        out_shape=(half, half),
        in_specs=[smem()] + [vmem()] * (4 + len(pieces) + len(parts)),
        out_specs=(vmem(), vmem()),
        scratch_shapes=[pltpu.VMEM((length, width), BF16)],
        compiler_params=params(),
        cost_estimate=cost(3),
        name="final_part",
    )(place, attended, lse, gated, w_own, *pieces, *parts)


def pair_kernel(place, tokens, keep, got, mine, away):
    spot = lax.div(place[1], 2)
    mine[...] = tokens[...].astype(F32) + (keep[spot].astype(F32) + got[spot].astype(F32))
    for step in range(1, keep.shape[0]):
        other = jnp.bitwise_xor(spot, step)
        away[step - 1] = (keep[other].astype(F32) + got[other].astype(F32)).astype(BF16)


def pair_sum(place, tokens, keep, got):
    count, length, width = keep.shape
    return pl.pallas_call(
        pair_kernel,
        out_shape=(
            jax.ShapeDtypeStruct((length, width), F32),
            jax.ShapeDtypeStruct((count - 1, length, width), BF16),
        ),
        in_specs=[smem()] + [vmem()] * 3,
        out_specs=(vmem(), vmem()),
        compiler_params=params(),
        cost_estimate=cost(1),
        name="pair_sum",
    )(place, tokens, keep, got)


def shards(tokens, norm_gain, w_attn, persist_kv, kv_pool, cache_len, mem_state, decay, rate):
    req, row, col = lax.axis_size("req"), lax.axis_size("row"), lax.axis_size("col")
    pool_size = req * row
    my_req, my_row, my_col = lax.axis_index("req"), lax.axis_index("row"), lax.axis_index("col")
    my_index = my_req * row + my_row
    length = tokens.shape[0]
    width = w_attn.shape[2]
    slots, page = kv_pool.shape[2], kv_pool.shape[3]

    def shift(x, axis, by, name):
        size = lax.axis_size(axis)
        with jax.named_scope(name):
            return lax.ppermute(x, axis, [(i, (i + by) % size) for i in range(size)])

    def after(x, *others):
        return lax.optimization_barrier((x,) + others)[0]

    w_query = w_attn[0]
    query_shards = [w_query] + [
        shift(w_query, "row", s, f"query_weights_{s}") for s in range(1, row)
    ]
    xfloat = tokens.astype(F32)
    normed = (
        xfloat * lax.rsqrt(jnp.mean(xfloat * xfloat, axis=-1, keepdims=True) + 1e-05) * norm_gain
    ).astype(BF16)
    scales = jnp.stack([decay[0], rate[0]])
    own_width = tokens.shape[1] // col
    own_cols = lax.dynamic_slice_in_dim(tokens, my_col * own_width, own_width, 1)
    groups = min(req, 4) if OPT["groups"] else 1
    group = my_req % groups
    place = jnp.stack([my_row, my_col, group]).astype(jnp.int32)

    order = [0] + list(dict.fromkeys([s for s in (1, row - 1) if 0 < s < row] + list(range(1, row))))
    steps = jnp.asarray(order, jnp.int32)[:, None]
    turns = jnp.arange(req, dtype=jnp.int32)[None, :]
    blocks = (((my_req - turns) % req) * row + (my_row - steps) % row).reshape(-1)
    offsets = (my_index - blocks) % pool_size
    limits = cache_len[blocks]
    used = jnp.clip(
        ((limits + page - 1) // page - offsets + pool_size - 1) // pool_size, 0, slots
    )
    last = (used - 1) * pool_size + offsets
    info = jnp.stack([blocks, used, limits - last * page], axis=1).astype(jnp.int32)

    pages = kv_pool[0].reshape(pool_size, slots * page, 2, width)
    place, scales, own_cols = lax.optimization_barrier((place, scales, own_cols))
    if OPT["lay"] == 1:
        pages = load_pages(info, pages, slots)
        place = after(place, *pages)
    queries = project(place, normed, query_shards)
    if OPT["lay"] == 2:
        pages = load_pages(after(info, queries), pages, slots)

    order = order[1:]
    far = order[-1]
    numbered = {}
    for s in [0] + order:
        for t in range(req):
            numbered[s, t] = len(numbered)
    partials, back, arrived = {}, {}, {}
    latest = [queries]
    outs = []

    def attend(s, t, here, parts=()):
        number = numbered[s, t]
        info_now = after(info, latest[0]) if OPT["kchain"] else info
        latest[0] = partials[s, t] = pool_attend(
            number, info_now, here, pages[number], parts, slots, page
        )
        outs.append(latest[0])

    def send_back(s, *first):
        back[s] = [
            shift(after(partials[s, t], *first), "req", -t, f"partials_req_{s}")
            for t in range(1, req)
        ]

    def merge_arrived(s, *first):
        if (s, 0) not in partials:
            attend(s, 0, after(by_row[s], *first), back[s])
            arrived[s] = latest[0]
            return
        if OPT["kchain"]:
            first = (latest[0],) + first
        parts = [after(partials[s, 0], *first)] + back[s]
        latest[0] = arrived[s] = merge_parts(parts, length, width)

    def over_row(x, name, relay, *first):
        got = {}
        for s in order:
            if s in (1, row - 1) or not relay:
                got[s] = shift(x, "row", s, f"{name}_row_{s}")
            else:
                moved = after(got[s - 1], *first)
                got[s] = shift(moved, "row", 1, f"{name}_row_{s}")
        return got

    def over_req(x, name, *first):
        return [shift(after(x, *first), "req", t, name) for t in range(1, req)]

    by_row = over_row(queries, "queries", OPT["relayq"])
    by_row[0] = queries
    there = {0: over_req(queries, "queries_req_0")}
    sequence = [(0, 0)] + [(0, t) for t in range(1, req)]
    if OPT["korder"] == 0:
        for s in order:
            sequence += [(s, t) for t in range(req)]
    elif OPT["korder"] == 1:
        sequence += [(s, 0) for s in order[:-1]]
        sequence += [(s, t) for s in order[:-1] for t in range(1, req)]
        sequence += [(order[-1], t) for t in range(req)]
    elif OPT["korder"] >= 4:
        one, near = order[0], order[1:-1]
        sequence = [(0, 0), (one, 0)] + [(0, t) for t in range(1, req)]
        sequence += [(one, t) for t in range(1, req)]
        if OPT["korder"] == 6:
            sequence += [(s, t) for s in near + [far] for t in range(1, req)]
            sequence += [(s, 0) for s in near + [far]]
        elif OPT["korder"] == 7:
            sequence += [(s, t) for s in [far] + near for t in range(1, req)]
            sequence += [(s, 0) for s in near + [far]]
        elif OPT["korder"] == 4:
            sequence += [(far, 0)] + [(s, t) for s in near for t in range(req)]
            sequence += [(far, t) for t in range(1, req)]
        else:
            sequence += [(s, 0) for s in near] + [(far, 0)]
            sequence += [(far, t) for t in range(1, req)]
            sequence += [(s, t) for s in near for t in range(1, req)]
    elif OPT["korder"] == 2:
        sequence = [(0, 0)] + [(s, 0) for s in order[:1]] + [(0, t) for t in range(1, req)]
        sequence += [(s, t) for s in order[:1] for t in range(1, req)]
        for s in order[1:]:
            sequence += [(s, t) for t in range(req)]
    else:
        sequence = [(0, 0)] + [(s, 0) for s in order[:1]]
        sequence += [(s, t) for s in order[:1] for t in range(1, req)]
        for s in order[1:]:
            sequence += [(s, t) for t in range(req)]
        sequence += [(0, t) for t in range(1, req)]
    fused = order[len(order) - OPT["fuse"] :]
    sequence = [(s, t) for s, t in sequence if t or s not in fused]
    when = {0: -1}
    for i, s in enumerate(order):
        when[s] = i
    for i, (s, t) in enumerate(sequence):
        if i == 1:
            first = outs if OPT["rtie"] == 1 else pages if OPT["rtie"] == 2 else []
            for f in range(2, row - 1):
                moved = after(by_row[f - 1], *first)
                by_row[f] = shift(moved, "row", 1, f"queries_row_{f}")
        if t and s not in there:
            first = []
            if OPT["ytie"] and when[s] >= 0:
                first = [outs[min(when[s], i - 1)]]
                if OPT["ytie"] == 2:
                    first = [outs[{order[0]: 0, far: 3}.get(s, 1)]]
                if OPT["ytie"] == 4:
                    first = [outs[0]]
                if OPT["ytie"] == 5:
                    first = [outs[{far: 0}.get(s, 1)]]
                if OPT["ytie"] == 6:
                    first = [outs[1]]
                if OPT["ytie"] == 3:
                    first = [outs[{order[0]: 0, far: 2}.get(s, 1)]]
            there[s] = over_req(by_row[s], f"queries_req_{s}", *first)
            if OPT["ytie"] > 1 and s == order[0]:
                for other in order[1:]:
                    if OPT["ytie"] < 4 and other == far:
                        continue
                    late = OPT["ytie"] < 4 or (OPT["ytie"] == 5 and other != far)
                    first = [outs[1 if late or OPT["ytie"] == 6 else 0]]
                    there[other] = over_req(by_row[other], f"queries_req_{other}", *first)
        attend(s, t, there[s][t - 1] if t else by_row[s])
    for s in order:
        first = []
        if OPT["ptie"] and s == far:
            first = [part for done in order[:-1] for part in back[done]]
        send_back(s, *first)

    share = 4 // groups
    w_share = lax.dynamic_slice_in_dim(w_attn, 1 + group * share, share, 0)
    ties = dict(
        q=[queries],
        near=[by_row[order[0]]],
        near2=[by_row[s] for s in order[:2]],
        far=[by_row[far]],
        all=[by_row[s] for s in order] + [outs[2]],
        k4=[outs[min(4, len(outs) - 1)]],
    )
    fetched = over_row(after(w_share, *ties[OPT["wtie"]]), "weights", OPT["relayw"])
    pieces = []
    for s in range(1, row):
        moved = fetched[s]
        if OPT["wytie"] == 1:
            moved = after(moved, outs[-1])
        elif OPT["wytie"] == 2:
            moved = after(moved, *back[far])
        elif OPT["wytie"] == 3 and s not in (1, row - 1):
            moved = after(moved, *back[far])
        pieces += [fetched[s]] + [
            shift(moved, "req", t, f"weights_req_{s}") for t in range(1, groups)
        ]
    for s in order if OPT["morder"] == 0 else order[::-1]:
        first = []
        if OPT["mtie"] == 1 and s == order[0]:
            first = [fetched[far]]
        if OPT["mtie"] == 2 and s == far:
            first = [fetched[far]]
        if OPT["wk"] and s == far:
            first = first + [pieces[groups * k + 1] for k in (0, row - 2)[: OPT["wk"]] if groups > 1]
        if OPT["ztie"] and s == far and s != order[0]:
            first = first + [arrived[order[0]]]
        merge_arrived(s, *first)
        merged_last = latest[0]
        arrived[s] = shift(arrived[s], "row", -s, f"partials_row_{s}")
    send_back(0, *([merged_last] if OPT["p0"] == 1 else [] if OPT["p0"] == 0 else [outs[-1]]))
    if not OPT["loc"]:
        merged_last = queries

    local_out, local_lse, recalled, new_state = local_part(
        place,
        scales,
        normed,
        after(queries, merged_last),
        persist_kv,
        mem_state,
        w_attn,
        pieces,
        row,
    )
    early = [partials[0, 0]] + back[0] + [arrived[s] for s in order[:-1]]
    mixed, lse, gated = early_part(
        place, normed, w_attn, pieces, row, recalled, local_out, local_lse, early
    )
    send, keep = final_part(place, mixed, lse, gated, [arrived[far]], w_attn, pieces, row)
    with jax.named_scope("output_pairs"):
        got = lax.ppermute(send, "col", [(i, i ^ 1) for i in range(col)])
    mine, away = pair_sum(place, own_cols, keep, got)
    for step in range(1, col // 2):
        with jax.named_scope("output_quarters"):
            came = lax.ppermute(away[step - 1], "col", [(i, i ^ (2 * step)) for i in range(col)])
        mine = mine + came.astype(F32)
    return (mine.astype(BF16), new_state)


def solution(mesh):
    return jax.shard_map(
        shards,
        mesh=mesh,
        in_specs=(
            P(("req", "row"), None),
            P(),
            P(None, "row", "col"),
            P(None, None, "col"),
            P(("req", "row"), None, None, None, None, "col"),
            P(),
            P(("req", "row"), "col", None, None),
            P(("req", "row"), None, "col"),
            P(("req", "row"), None, "col"),
        ),
        out_specs=(P(("req", "row"), "col"), P(("req", "row"), "col", None, None)),
        check_vma=False,
    )
```
